32 devices in a mesh: leaf: 4 (over y, x), box: 8 (over z, core).
Axes of the slice: x: 2, y: 2, z: 4, core: 2. Of those that a mesh axis runs over, the one named last changes fastest.
Arguments:
- krylov_block: float32 [64, 32768], P(None, ('leaf', 'box')), as said below
- bases: float32 [32, 32768], P(None, ('leaf', 'box')), may hold values from -0.5 to 0.5
- points: float32 [3, 32768], P(None, ('leaf', 'box')), may hold values from 0 to 1, as said below
- panel_size: float32 [32768], P(('leaf', 'box')), may hold values from 0.002 to 0.008
- panel_weight: float32 [32768], P(('leaf', 'box')), may hold values from 0.5 to 2
- near_list: int32 [256, 16], P(('leaf', 'box')), may hold values from 0 to 255, as said below
- far_list: int32 [256, 12], P(('leaf', 'box')), may hold values from 0 to 255, as said below
- far_class: int32 [256, 12], P(('leaf', 'box')), may hold values from 0 to 15
- far_count: int32 [256], P(('leaf', 'box')), may hold values from 1 to 12
- coarse_list: int32 [32, 16], P(('leaf', 'box')), may hold values from 0 to 31, as said below
- coarse_class: int32 [32, 16], P(('leaf', 'box')), may hold values from 0 to 15
- coarse_count: int32 [32], P(('leaf', 'box')), may hold values from 1 to 16
- couple_fine: float32 [16, 32, 32], replicated, may hold values from -0.3125 to 0.3125
- couple_coarse: float32 [16, 32, 32], replicated, may hold values from -1 to 1
- up_transfer: float32 [8, 32, 32], replicated, may hold values from -0.375 to 0.375
- down_transfer: float32 [8, 32, 32], replicated, may hold values from -1 to 1
Outputs:
- basis_next: float32 [64, 32768], P(None, ('leaf', 'box'))
- hessenberg: float32 [64, 64], replicated
- factor: float32 [64, 64], replicated
The draws below stay inside these ranges and needn't reach their ends.
Inputs may be any that keep to these rules, and one draw needn't show every extreme that they name: `near_list`: entry 0 of a box's row is the box itself. Every entry lies in the box's own group of 64 consecutive boxes (groups aligned), and at most 8 boxes before the first or after the last box of the box's aligned block of 8 boxes. `far_list`: every entry lies in the box's own aligned group of 64 consecutive boxes. `coarse_list`: entries may name any parent. `krylov_block`: rows differ in scale. `points`: the panels of leaf box b lie in the cell of a regular grid of the unit cube that the Morton code b names (bit k of b counts along coordinate k mod 3).
All inputs are finite; a program needn't handle non-finite values.
Results may differ from the reference program's by a relative error of at most 0.0025.
Values sent between devices are 32-bit elements; how exact they have to be, the bound alone decides.
A program may use at most 64 MiB of HBM per device.

```python
import math
import jax
import jax.numpy as jnp
from jax import lax

RHS = 64
RANK = 32
M = 128
CHILDREN = 8
NEAR = 16
FAR1 = 12
FAR2 = 16
CLASSES = 16
PARENTS = 32
BOXES = 256
SUB_BOXES = 64
PANELS = 32768


def draw_krylov_block(key, part):
    position = jnp.arange(PANELS, dtype=jnp.float32) / PANELS
    return jax.random.normal(key, (RHS, PANELS), jnp.float32) * (1.0 + 2.0 * position)


def draw_points(key, part):
    box_ids = jnp.arange(PANELS, dtype=jnp.int32) // M
    bit_total = BOXES.bit_length() - 1
    cells = [jnp.zeros((PANELS,), jnp.int32) for axis_number in range(3)]
    extents = [1, 1, 1]
    for bit_number in range(bit_total):
        axis_number = bit_number % 3
        bit_value = box_ids // 2 ** bit_number % 2
        cells[axis_number] = cells[axis_number] + bit_value * 2 ** (bit_number // 3)
        extents[axis_number] = extents[axis_number] * 2
    inside = jax.random.uniform(jax.random.fold_in(key, 31), (3, PANELS), jnp.float32, 0.0, 1.0)
    rows = [(cells[axis_number].astype(jnp.float32) + inside[axis_number]) / extents[axis_number] for axis_number in range(3)]
    return jnp.clip(jnp.stack(rows, 0), 0.0, 1.0)


def draw_near_list(key, part):
    box_ids = jnp.arange(BOXES, dtype=jnp.int32)
    block_first = box_ids // CHILDREN * CHILDREN
    group_first = box_ids // SUB_BOXES * SUB_BOXES
    offsets = jax.random.randint(jax.random.fold_in(key, 11), (BOXES, NEAR - 1), 0, 3 * CHILDREN, dtype=jnp.int32)
    candidate = block_first[:, None] - CHILDREN + offsets
    candidate = jnp.clip(candidate, group_first[:, None], group_first[:, None] + SUB_BOXES - 1)
    return jnp.concatenate([box_ids[:, None], candidate], axis=1).astype(jnp.int32)


def draw_far_list(key, part):
    box_ids = jnp.arange(BOXES, dtype=jnp.int32)
    group_first = box_ids // SUB_BOXES * SUB_BOXES
    offsets = jax.random.randint(jax.random.fold_in(key, 23), (BOXES, FAR1), 0, SUB_BOXES, dtype=jnp.int32)
    return (group_first[:, None] + offsets).astype(jnp.int32)


def draw_coarse_list(key, part):
    parent_ids = jnp.arange(PARENTS, dtype=jnp.int32)
    previous = (parent_ids + PARENTS - 1) % PARENTS
    opposite = (parent_ids + PARENTS // 2) % PARENTS
    others = jax.random.randint(jax.random.fold_in(key, 37), (PARENTS, FAR2 - 2), 0, PARENTS, dtype=jnp.int32)
    return jnp.concatenate([previous[:, None], opposite[:, None], others], axis=1).astype(jnp.int32)


def plant(entries, stream_key, low, high):
    shape = entries.shape
    spot = [jax.random.randint(jax.random.fold_in(stream_key, axis), (), 0, shape[axis]) for axis in range(len(shape))]
    entries = entries.at[tuple(spot)].set(low)
    longest = shape.index(max(shape))
    spot[longest] = (spot[longest] + 1) % shape[longest]
    return entries.at[tuple(spot)].set(high)


def shard_levels(stream_key, dims, cuts, least, largest):
    def one(dim, shards_of):
        steps = jax.random.uniform(jax.random.fold_in(jax.random.fold_in(stream_key, 6), dim), (shards_of,), jnp.float32, least / len(cuts), largest / len(cuts))
        return jnp.repeat(jnp.exp(steps), dims[dim] // shards_of).reshape((-1,) + (1,) * (len(dims) - dim - 1))

    loudness = one(*cuts[0])
    for cut in cuts[1:]:
        loudness = loudness * one(*cut)
    return loudness


def noise(rng, extent, scale, most, pieces=(), held_as=jnp.bfloat16):
    values = scale * jax.random.normal(rng, extent, jnp.float32)
    if pieces:
        values = values * shard_levels(rng, extent, pieces, -0.22, 0.18)
    return jnp.clip(values, -most, most).astype(held_as)


def setup_inputs(seed: int = 0) -> dict:
    key_list = jax.random.split(jax.random.key(seed), 17)
    return {
        "krylov_block": draw_krylov_block(jax.random.fold_in(key_list[16], 71), 0),
        "bases": noise(key_list[1], (RANK, PANELS), M ** -0.5, 0.5, ((1, 32),), jnp.float32),
        "points": draw_points(jax.random.fold_in(key_list[16], 71), 0),
        "panel_size": jnp.clip(jnp.exp(math.log(0.008) - 1.3862944 * jax.random.uniform(key_list[3], (PANELS,), jnp.float32) ** shard_levels(key_list[3], (PANELS,), ((0, 32),), -0.2, 0.2)), 0.002, 0.008),
        "panel_weight": jnp.clip(jnp.exp(math.log(2.0) - 1.3862944 * jax.random.uniform(key_list[4], (PANELS,), jnp.float32) ** shard_levels(key_list[4], (PANELS,), ((0, 32),), -0.2, 0.2)), 0.5, 2.0),
        "near_list": draw_near_list(jax.random.fold_in(key_list[16], 71), 0),
        "far_list": draw_far_list(jax.random.fold_in(key_list[16], 71), 0),
        "far_class": plant(jax.random.randint(key_list[7], (BOXES, FAR1), 0, CLASSES), jax.random.fold_in(key_list[7], 1), 0, CLASSES - 1).astype(jnp.int32),
        "far_count": plant(jax.random.randint(key_list[8], (BOXES,), 1, FAR1 + 1), jax.random.fold_in(key_list[8], 1), 1, FAR1).astype(jnp.int32),
        "coarse_list": draw_coarse_list(jax.random.fold_in(key_list[16], 71), 0),
        "coarse_class": plant(jax.random.randint(key_list[10], (PARENTS, FAR2), 0, CLASSES), jax.random.fold_in(key_list[10], 1), 0, CLASSES - 1).astype(jnp.int32),
        "coarse_count": plant(jax.random.randint(key_list[11], (PARENTS,), 1, FAR2 + 1), jax.random.fold_in(key_list[11], 1), 1, FAR2).astype(jnp.int32),
        "couple_fine": noise(key_list[12], (CLASSES, RANK, RANK), (RANK * FAR1) ** -0.5, 0.3125, (), jnp.float32),
        "couple_coarse": noise(key_list[13], (CLASSES, RANK, RANK), RANK ** -0.5, 1.0, (), jnp.float32),
        "up_transfer": noise(key_list[14], (CHILDREN, RANK, RANK), (RANK * CHILDREN) ** -0.5, 0.375, (), jnp.float32),
        "down_transfer": noise(key_list[15], (CHILDREN, RANK, RANK), RANK ** -0.5, 1.0, (), jnp.float32),
    }


HIGHEST_PRECISION = lax.Precision.HIGHEST

def pairwise(target, source, source_values, scale_count):
    first = target[0][:, None] - source[0][None, :]
    second = target[1][:, None] - source[1][None, :]
    third = target[2][:, None] - source[2][None, :]
    squared = first * first + second * second + third * third
    green = source[4][None, :] / (scale_count * jnp.sqrt(squared + target[3][:, None] * source[3][None, :]))
    return jnp.dot(source_values, green.T, precision=HIGHEST_PRECISION)

def reference(krylov_block, bases, points, panel_size, panel_weight, near_list, far_list, far_class, far_count, coarse_list, coarse_class, coarse_count, couple_fine, couple_coarse, up_transfer, down_transfer):
    block_values = krylov_block.reshape(RHS, BOXES, M)
    block_basis = bases.reshape(RANK, BOXES, M)
    geometry = jnp.concatenate([points, panel_size[None, :], panel_weight[None, :]], 0).reshape(5, BOXES, M)
    fine_poles = jnp.einsum('rbm,qbm->brq', block_basis, block_values, precision=HIGHEST_PRECISION)
    grouped = fine_poles.reshape(PARENTS, CHILDREN, RANK, RHS)
    coarse_poles = jnp.einsum('ckr,pckq->prq', up_transfer, grouped, precision=HIGHEST_PRECISION)
    live_coarse = (jnp.arange(FAR2, dtype=jnp.int32)[None, :] < coarse_count[:, None]).astype(jnp.float32)
    coarse_matrices = couple_coarse[coarse_class] * live_coarse[:, :, None, None]
    coarse_local = jnp.einsum('perk,pekq->prq', coarse_matrices, coarse_poles[coarse_list], precision=HIGHEST_PRECISION)

    def per_box(box_index):
        sources = near_list[box_index]
        source_geometry = geometry[:, sources].reshape(5, NEAR * M)
        source_values = block_values[:, sources].reshape(RHS, NEAR * M)
        near_field = pairwise(geometry[:, box_index], source_geometry, source_values, M * NEAR)
        live_mask = (jnp.arange(FAR1, dtype=jnp.int32) < far_count[box_index]).astype(jnp.float32)
        matrices = couple_fine[far_class[box_index]] * live_mask[:, None, None]
        fine_local = jnp.einsum('erk,ekq->rq', matrices, fine_poles[far_list[box_index]], precision=HIGHEST_PRECISION)
        fine_local = fine_local + jnp.dot(down_transfer[box_index % CHILDREN], coarse_local[box_index // CHILDREN], precision=HIGHEST_PRECISION)
        far_field = jnp.dot(fine_local.T, block_basis[:, box_index], precision=HIGHEST_PRECISION)
        return near_field + far_field
    product = lax.map(per_box, jnp.arange(BOXES, dtype=jnp.int32))
    product = product.transpose(1, 0, 2).reshape(RHS, PANELS)
    hessenberg = jnp.dot(krylov_block, product.T, precision=HIGHEST_PRECISION) / PANELS
    residual = product - jnp.dot(hessenberg.T, krylov_block, precision=HIGHEST_PRECISION)
    gram_matrix = jnp.dot(residual, residual.T, precision=HIGHEST_PRECISION) / PANELS
    factor = jnp.linalg.cholesky(gram_matrix)
    basis_next = lax.linalg.triangular_solve(factor, residual, left_side=True, lower=True)
    return (basis_next, hessenberg, factor)
```

```python
import functools

import jax
import jax.numpy as jnp
from jax import lax
from jax.experimental import pallas as pl
from jax.experimental.pallas import tpu as pltpu
from jax.sharding import PartitionSpec as P

HIGHEST = lax.Precision.HIGHEST
MESH = pl.DeviceIdType.MESH
F32 = jnp.float32
BF16 = jnp.bfloat16


def nn(a, b):
    return jnp.dot(a, b, precision=HIGHEST, preferred_element_type=F32)


def nt(a, b):
    return lax.dot_general(
        a, b, (((1,), (1,)), ((), ())), precision=HIGHEST, preferred_element_type=F32
    )


def split(x):
    high = x.astype(BF16)
    return high, (x - high.astype(F32)).astype(BF16)


def product_kernel(
    n_leaf, n_box, nb, width, scale,
    k_ref, b_ref, pts_ref, size_ref, weight_ref,
    near_ref, flist_ref, fclass_ref, fcount_ref, clist_ref, cclass_ref, ccount_ref,
    cf_ref, cc_ref, up_ref, down_ref,
    prod_ref, red_ref,
    ext_k, ext_g, kcat, geo_t, fbuf, cleaf, cbuf, fpole, cpole, tfine, tcoarse, dloc,
    rbuf, rrecv, lrecv, gath,
    nk_s, nk_r, ng_s, ng_r, f_s, f_r, ff_s, ff_r, c_s, c_r, cf_s, cf_r, cl_s, cl_r,
    r_s, r_r, l_s, l_r, g_s, g_r,
):
    q = k_ref.shape[0]
    r = b_ref.shape[0]
    leaf = lax.axis_index("leaf")
    box = lax.axis_index("box")
    nz = n_box // 2
    core = lax.rem(box, 2)
    z = box // 2
    sibling = 2 * z + (1 - core)
    near_count = near_ref.shape[1]
    far_count = flist_ref.shape[1]
    coarse_count = clist_ref.shape[1]
    first_box = (leaf * n_box + box) * nb
    group_first = leaf * n_box * nb

    barrier = pltpu.get_barrier_semaphore()
    for d in range(1, n_box):
        pl.semaphore_signal(
            barrier, inc=1, device_id=(leaf, lax.rem(box + d, n_box)), device_id_type=MESH
        )
    for d in range(1, n_leaf):
        pl.semaphore_signal(
            barrier, inc=1, device_id=(lax.rem(leaf + d, n_leaf), box), device_id_type=MESH
        )

    def remote(src, dst, s_sem, r_sem, dev):
        return pltpu.make_async_remote_copy(
            src_ref=src, dst_ref=dst, send_sem=s_sem, recv_sem=r_sem,
            device_id=dev, device_id_type=MESH,
        )

    weights = weight_ref[...] * (1.0 / scale)
    weighted = k_ref[...] * weights
    geo = jnp.concatenate(
        [pts_ref[...], size_ref[...], weight_ref[...], pts_ref[...]], axis=0
    )
    for b in range(nb):
        lanes = slice(b * width, (b + 1) * width)
        ext_k[nb + b] = weighted[:, lanes]
        ext_g[nb + b] = geo[:, lanes]
        geo_t[b] = geo[:, lanes].T

    pl.semaphore_wait(barrier, n_box - 1 + n_leaf - 1)

    right = (leaf, lax.rem(box + 1, n_box))
    left = (leaf, lax.rem(box + n_box - 1, n_box))
    own = pl.ds(nb, nb)
    low = pl.ds(0, nb)
    top = pl.ds(2 * nb, nb)
    k_right = remote(ext_k.at[own], ext_k.at[low], nk_s.at[0], nk_r.at[0], right)
    g_right = remote(ext_g.at[own], ext_g.at[low], ng_s.at[0], ng_r.at[0], right)
    k_left = remote(ext_k.at[own], ext_k.at[top], nk_s.at[1], nk_r.at[1], left)
    g_left = remote(ext_g.at[own], ext_g.at[top], ng_s.at[1], ng_r.at[1], left)

    @pl.when(box < n_box - 1)
    def _():
        k_right.start()
        g_right.start()

    @pl.when(box > 0)
    def _():
        k_left.start()
        g_left.start()

    @pl.when(box == 0)
    def _():
        ext_k[low] = jnp.zeros((nb, q, width), F32)
        ext_g[low] = jnp.zeros((nb, 8, width), F32)

    @pl.when(box == n_box - 1)
    def _():
        ext_k[top] = jnp.zeros((nb, q, width), F32)
        ext_g[top] = jnp.zeros((nb, 8, width), F32)

    poles = []
    for b in range(nb):
        lanes = slice(b * width, (b + 1) * width)
        poles.append(nt(b_ref[:, lanes], k_ref[:, lanes]))
    for h in range(nb // 2):
        fbuf[box, h * r : (h + 1) * r, :] = jnp.concatenate(
            [poles[2 * h], poles[2 * h + 1]], axis=1
        )

    def spread(buf, s_sems, r_sems, fs_sems, fr_sems):
        mine = buf.at[box]
        copies = [remote(mine, mine, fs_sems.at[0], fr_sems.at[0], (leaf, sibling))]
        for d in range(1, nz):
            peer = 2 * lax.rem(z + d, nz) + core
            copies.append(remote(mine, mine, s_sems.at[d], r_sems.at[d], (leaf, peer)))
        return copies

    def forward(buf, fs_sems, fr_sems):
        result = []
        for d in range(1, nz):
            source = 2 * lax.rem(z + nz - d, nz) + core
            slot = buf.at[source]
            result.append(remote(slot, slot, fs_sems.at[d], fr_sems.at[d], (leaf, sibling)))
        return result

    fine_out = spread(fbuf, f_s, f_r, ff_s, ff_r)
    for copy in fine_out:
        copy.start()

    cpole_own = nn(up_ref[...].T, jnp.concatenate(poles, axis=0))
    cleaf[leaf] = jnp.concatenate([cpole_own, cpole_own], axis=1)
    leaf_out = [
        remote(
            cleaf.at[leaf], cleaf.at[leaf], cl_s.at[d], cl_r.at[d],
            (lax.rem(leaf + d, n_leaf), box),
        )
        for d in range(1, n_leaf)
    ]
    for copy in leaf_out:
        copy.start()

    def to_split(i, carry):
        high, rest = split(ext_k[i])
        kcat[i] = jnp.concatenate([high, rest], axis=0)
        return carry

    lax.fori_loop(nb, 2 * nb, to_split, 0)
    lane4 = lax.broadcasted_iota(jnp.int32, (r, 4 * r), 1) // r
    for c in range(cf_ref.shape[0]):
        tfine[c] = jnp.concatenate([cf_ref[c]] * 4, axis=1)
    for c in range(cc_ref.shape[0]):
        tcoarse[c] = jnp.concatenate([cc_ref[c]] * 4, axis=1)

    for copy in leaf_out:
        copy.wait_recv()
    for h in range(n_leaf // 2):
        cbuf[box, h * r : (h + 1) * r, :] = jnp.concatenate(
            [cleaf[2 * h][:, :q], cleaf[2 * h + 1][:, :q]], axis=1
        )
    coarse_out = spread(cbuf, c_s, c_r, cf_s, cf_r)
    for copy in coarse_out:
        copy.start()

    @pl.when(box > 0)
    def _():
        k_right.wait_recv()
        g_right.wait_recv()

    @pl.when(box < n_box - 1)
    def _():
        k_left.wait_recv()
        g_left.wait_recv()

    lax.fori_loop(0, nb, to_split, 0)
    lax.fori_loop(2 * nb, 3 * nb, to_split, 0)

    shift = nb - first_box

    def near_box(b, carry):
        target = geo_t[b]
        columns = [jnp.broadcast_to(target[:, c : c + 1], (width, width)) for c in range(4)]

        def pair(t, total):
            greens = []
            sources = []
            for side in range(2):
                i = jnp.clip(near_ref[b, 2 * t + side] + shift, 0, 3 * nb - 1)
                g = ext_g[i]
                first = columns[0] - g[0:1]
                second = columns[1] - g[1:2]
                third = columns[2] - g[2:3]
                squared = first * first + second * second + third * third
                greens.append(lax.rsqrt(squared + columns[3] * g[3:4]))
                sources.append(kcat[i])
            high, rest = split(jnp.concatenate(greens, axis=1))
            both = jnp.concatenate([high, rest], axis=0)
            source = jnp.concatenate(sources, axis=1)
            return total + lax.dot_general(
                source, both, (((1,), (1,)), ((), ())), preferred_element_type=F32
            )

        total = lax.fori_loop(
            0, near_count // 2, pair, jnp.zeros((2 * q, 2 * width), F32)
        )
        half = total[:, :width] + total[:, width:]
        prod_ref[:, pl.ds(pl.multiple_of(b * width, width), width)] = half[:q] + half[q:]
        return carry

    def near_range(lo, hi):
        lax.fori_loop(lo, hi, near_box, 0)

    near_range(0, nb // 2)
    fine_fwd = forward(fbuf, ff_s, ff_r)
    for d in range(1, nz):
        fine_out[d].wait_recv()
        fine_fwd[d - 1].start()
    coarse_fwd = forward(cbuf, cf_s, cf_r)
    for d in range(1, nz):
        coarse_out[d].wait_recv()
        coarse_fwd[d - 1].start()
    near_range(nb // 2, nb)

    for copy in [coarse_out[0]] + coarse_fwd + [fine_out[0]] + fine_fwd:
        copy.wait_recv()

    def open_coarse(i, carry):
        for h in range(n_leaf // 2):
            rows = cbuf[i, h * r : (h + 1) * r, :]
            cpole[2 * h * n_box + i] = rows[:, :q]
            cpole[(2 * h + 1) * n_box + i] = rows[:, q:]
        return carry

    lax.fori_loop(0, n_box, open_coarse, 0)

    def open_fine(i, carry):
        for h in range(nb // 2):
            rows = fbuf[i, h * r : (h + 1) * r, :]
            fpole[i * nb + 2 * h] = rows[:, :q]
            fpole[i * nb + 2 * h + 1] = rows[:, q:]
        return carry

    lax.fori_loop(0, n_box, open_fine, 0)

    def coupled(table, class_of, pole, index_of, live, entries):
        left_side = []
        for group in range(entries // 4):
            block = None
            for side in range(4):
                e = 4 * group + side
                mask = jnp.where(e < live, 1.0, 0.0).astype(F32)
                piece = table[class_of(e)] * mask
                block = piece if side == 0 else jnp.where(lane4 == side, piece, block)
            left_side.append(block)
        right_side = [pole[index_of(e)] for e in range(entries)]
        return nn(jnp.concatenate(left_side, axis=1), jnp.concatenate(right_side, axis=0))

    coarse_local = coupled(
        tcoarse, lambda e: cclass_ref[0, e], cpole, lambda e: clist_ref[0, e],
        ccount_ref[0], coarse_count,
    )
    lowered = nn(down_ref[...], coarse_local)
    for b in range(nb):
        dloc[b] = lowered[b * r : (b + 1) * r]

    def far_box(b, carry):
        local = dloc[b] + coupled(
            tfine, lambda e: fclass_ref[b, e], fpole,
            lambda e: jnp.clip(flist_ref[b, e] - group_first, 0, n_box * nb - 1),
            fcount_ref[b], far_count,
        )
        lanes = pl.ds(pl.multiple_of(b * width, width), width)
        prod_ref[:, lanes] = prod_ref[:, lanes] + nn(local.T, b_ref[:, lanes])
        return carry

    lax.fori_loop(0, nb, far_box, 0)

    stacked = jnp.concatenate([k_ref[...], prod_ref[...]], axis=0)
    gram = nt(stacked, stacked)
    share = rbuf.shape[1]
    for s in range(n_box):
        rbuf[s] = gram[s * share : (s + 1) * share]
    r_out = []
    for d in range(1, n_box):
        peer = lax.rem(box + d, n_box)
        r_out.append(
            remote(rbuf.at[peer], rrecv.at[box], r_s.at[d], r_r.at[d], (leaf, peer))
        )
        r_out[-1].start()
    rrecv[box] = rbuf[box]
    for copy in r_out:
        copy.wait_recv()
    part = rrecv[0]
    for s in range(1, n_box):
        part = part + rrecv[s]
    lrecv[leaf] = part
    l_out = []
    for d in range(1, n_leaf):
        peer = lax.rem(leaf + d, n_leaf)
        l_out.append(
            remote(lrecv.at[leaf], lrecv.at[leaf], l_s.at[d], l_r.at[d], (peer, box))
        )
        l_out[-1].start()
    for copy in l_out:
        copy.wait_recv()
    part = lrecv[0]
    for s in range(1, n_leaf):
        part = part + lrecv[s]
    gath[box] = part
    g_out = []
    for d in range(1, n_box):
        peer = lax.rem(box + d, n_box)
        g_out.append(remote(gath.at[box], gath.at[box], g_s.at[d], g_r.at[d], (leaf, peer)))
        g_out[-1].start()
    for copy in g_out:
        copy.wait_recv()
    red_ref[...] = gath[...]

    @pl.when(box < n_box - 1)
    def _():
        k_right.wait_send()
        g_right.wait_send()

    @pl.when(box > 0)
    def _():
        k_left.wait_send()
        g_left.wait_send()

    for copy in fine_out + fine_fwd + leaf_out + coarse_out + coarse_fwd + r_out + l_out + g_out:
        copy.wait_send()


def finish_kernel(panels, k_ref, prod_ref, red_ref, basis_ref, hess_ref, factor_ref):
    q = k_ref.shape[0]
    red = red_ref[...]
    basis_gram = red[:q, :q]
    mixed = red[:q, q:]
    mixed_t = red[q:, :q]
    image = red[q:, q:]
    inverse = 1.0 / panels
    hess = mixed * inverse
    hess_t = mixed_t * inverse
    hess_ref[...] = hess
    corrected = image - nn(mixed_t, hess) - nn(hess_t, mixed)
    corrected = (corrected + nn(nn(hess_t, basis_gram), hess)) * inverse
    eye = (
        lax.broadcasted_iota(jnp.int32, (q, q), 0) == lax.broadcasted_iota(jnp.int32, (q, q), 1)
    ).astype(F32)
    start = jnp.concatenate([corrected, eye], axis=1)
    tiles = [start[8 * t : 8 * t + 8] for t in range(q // 8)]
    row_id = lax.broadcasted_iota(jnp.int32, (8, 2 * q), 0)
    for p in range(q // 8):
        cols = [
            [jnp.broadcast_to(tiles[t][:, 8 * p + c : 8 * p + c + 1], (8, 2 * q)) for t in range(p, q // 8)]
            for c in range(8)
        ]
        for c in range(8):
            pivot = cols[c][0][c : c + 1]
            scale = lax.rsqrt(pivot)
            row = tiles[p][c : c + 1] * scale
            scaled = [tile * scale for tile in cols[c]]
            scaled[0] = jnp.where(row_id > c, scaled[0], 0.0)
            for j in range(c + 1, 8):
                value = cols[j][0][c : c + 1] * scale
                cols[j] = [x - s * value for x, s in zip(cols[j], scaled)]
            tiles[p] = jnp.where(row_id == c, row, tiles[p] - scaled[0] * row)
            for t in range(p + 1, q // 8):
                tiles[t] = tiles[t] - scaled[t - p] * row
    done = jnp.concatenate(tiles, axis=0)
    lower = done[:, :q].T
    keep = lax.broadcasted_iota(jnp.int32, (q, q), 0) >= lax.broadcasted_iota(jnp.int32, (q, q), 1)
    factor_ref[...] = jnp.where(keep, lower, 0.0)
    solve = jnp.where(keep, done[:, q:], 0.0)
    residual = prod_ref[...] - nn(hess_t, k_ref[...])
    basis_ref[...] = nn(solve, residual)


def per_device(
    krylov_block, bases, points, panel_size, panel_weight, near_list, far_list, far_class,
    far_count, coarse_list, coarse_class, coarse_count, couple_fine, couple_coarse,
    up_transfer, down_transfer,
):
    q, local = krylov_block.shape
    r = bases.shape[0]
    nb = near_list.shape[0]
    width = local // nb
    n_leaf = lax.axis_size("leaf")
    n_box = lax.axis_size("box")
    nz = n_box // 2
    share = 2 * q // n_box
    panels = local * n_leaf * n_box
    vmem = pl.BlockSpec(memory_space=pltpu.VMEM)
    smem = pl.BlockSpec(memory_space=pltpu.SMEM)
    dma = lambda n: pltpu.SemaphoreType.DMA((n,))
    product, reduced = pl.pallas_call(
        functools.partial(
            product_kernel, n_leaf, n_box, nb, width, float(width * near_list.shape[1])
        ),
        out_shape=(
            jax.ShapeDtypeStruct((q, local), F32),
            jax.ShapeDtypeStruct((n_box, share, 2 * q), F32),
        ),
        in_specs=[vmem] * 5 + [smem] * 7 + [vmem] * 4,
        out_specs=(vmem, vmem),
        scratch_shapes=[
            pltpu.VMEM((3 * nb, q, width), F32),
            pltpu.VMEM((3 * nb, 8, width), F32),
            pltpu.VMEM((3 * nb, 2 * q, width), BF16),
            pltpu.VMEM((nb, width, 8), F32),
            pltpu.VMEM((n_box, nb // 2 * r, 2 * q), F32),
            pltpu.VMEM((n_leaf, r, 2 * q), F32),
            pltpu.VMEM((n_box, n_leaf // 2 * r, 2 * q), F32),
            pltpu.VMEM((n_box * nb, r, q), F32),
            pltpu.VMEM((n_box * n_leaf, r, q), F32),
            pltpu.VMEM((couple_fine.shape[0], r, 4 * r), F32),
            pltpu.VMEM((couple_coarse.shape[0], r, 4 * r), F32),
            pltpu.VMEM((nb, r, q), F32),
            pltpu.VMEM((n_box, share, 2 * q), F32),
            pltpu.VMEM((n_box, share, 2 * q), F32),
            pltpu.VMEM((n_leaf, share, 2 * q), F32),
            pltpu.VMEM((n_box, share, 2 * q), F32),
            dma(2), dma(2), dma(2), dma(2),
            dma(nz), dma(nz), dma(nz), dma(nz),
            dma(nz), dma(nz), dma(nz), dma(nz),
            dma(n_leaf), dma(n_leaf),
            dma(n_box), dma(n_box), dma(n_leaf), dma(n_leaf), dma(n_box), dma(n_box),
        ],
        compiler_params=pltpu.CompilerParams(
            collective_id=0, has_side_effects=True, vmem_limit_bytes=48 * 2**20
        ),
    )(
        krylov_block, bases, points, panel_size[None, :], panel_weight[None, :],
        near_list, far_list, far_class, far_count, coarse_list, coarse_class, coarse_count,
        couple_fine, couple_coarse,
        up_transfer.reshape(-1, r), down_transfer.reshape(-1, r),
    )
    return pl.pallas_call(
        functools.partial(finish_kernel, float(panels)),
        out_shape=(
            jax.ShapeDtypeStruct((q, local), F32),
            jax.ShapeDtypeStruct((q, q), F32),
            jax.ShapeDtypeStruct((q, q), F32),
        ),
        in_specs=[vmem] * 3,
        out_specs=(vmem, vmem, vmem),
        compiler_params=pltpu.CompilerParams(vmem_limit_bytes=32 * 2**20),
    )(krylov_block, product, reduced.reshape(2 * q, 2 * q))


def solution(mesh):
    split_last = P(None, ("leaf", "box"))
    split_first = P(("leaf", "box"), None)
    flat = P(("leaf", "box"))
    in_specs = (
        split_last, split_last, split_last, flat, flat,
        split_first, split_first, split_first, flat,
        split_first, split_first, flat,
        P(), P(), P(), P(),
    )
    return jax.shard_map(
        per_device, mesh=mesh, in_specs=in_specs, out_specs=(split_last, P(), P()),
        check_vma=False,
    )
```

```python
import functools

import jax
import jax.numpy as jnp
from jax import lax
from jax.experimental import pallas as pl
from jax.experimental.pallas import tpu as pltpu
from jax.sharding import PartitionSpec as P

HIGHEST = lax.Precision.HIGHEST
MESH = pl.DeviceIdType.MESH
F32 = jnp.float32
BF16 = jnp.bfloat16


def nn(a, b):
    return jnp.dot(a, b, precision=HIGHEST, preferred_element_type=F32)


def nt(a, b):
    return lax.dot_general(
        a, b, (((1,), (1,)), ((), ())), precision=HIGHEST, preferred_element_type=F32
    )


def split(x):
    high = x.astype(BF16)
    return high, (x - high.astype(F32)).astype(BF16)


def product_kernel(
    n_leaf, n_box, nb, width, scale,
    k_ref, b_ref, pts_ref, size_ref, weight_ref,
    near_ref, flist_ref, fclass_ref, fcount_ref, clist_ref, cclass_ref, ccount_ref,
    cf_ref, cc_ref, up_ref, down_ref,
    prod_ref, red_ref,
    ext_k, ext_g, kcat, geo_t, greens, fbuf, lbuf, fpole, cpole, tfine, tcoarse, dloc,
    rbuf, rrecv, lrecv, gath,
    nk_s, nk_r, ng_s, ng_r, f_s, f_r, ff_s, ff_r, cl_s, cl_r,
    r_s, r_r, l_s, l_r, g_s, g_r,
):
    q = k_ref.shape[0]
    r = b_ref.shape[0]
    leaf = lax.axis_index("leaf")
    box = lax.axis_index("box")
    nz = n_box // 2
    core = lax.rem(box, 2)
    z = box // 2
    sibling = 2 * z + (1 - core)
    near_count = near_ref.shape[1]
    far_count = flist_ref.shape[1]
    coarse_count = clist_ref.shape[1]
    first_box = (leaf * n_box + box) * nb
    group_first = leaf * n_box * nb

    barrier = pltpu.get_barrier_semaphore()
    for d in range(1, n_box):
        pl.semaphore_signal(
            barrier, inc=1, device_id=(leaf, lax.rem(box + d, n_box)), device_id_type=MESH
        )
    for d in range(1, n_leaf):
        pl.semaphore_signal(
            barrier, inc=1, device_id=(lax.rem(leaf + d, n_leaf), box), device_id_type=MESH
        )

    def remote(src, dst, s_sem, r_sem, dev):
        return pltpu.make_async_remote_copy(
            src_ref=src, dst_ref=dst, send_sem=s_sem, recv_sem=r_sem,
            device_id=dev, device_id_type=MESH,
        )

    weights = weight_ref[...] * (1.0 / scale)
    weighted = k_ref[...] * weights
    geo = jnp.concatenate(
        [pts_ref[...], size_ref[...], weight_ref[...], pts_ref[...]], axis=0
    )
    for b in range(nb):
        lanes = slice(b * width, (b + 1) * width)
        ext_k[nb + b] = weighted[:, lanes]
        ext_g[nb + b] = geo[:, lanes]
        geo_t[b] = geo[:, lanes].T

    pl.semaphore_wait(barrier, n_box - 1 + n_leaf - 1)

    right = (leaf, lax.rem(box + 1, n_box))
    left = (leaf, lax.rem(box + n_box - 1, n_box))
    own = pl.ds(nb, nb)
    low = pl.ds(0, nb)
    top = pl.ds(2 * nb, nb)
    k_right = remote(ext_k.at[own], ext_k.at[low], nk_s.at[0], nk_r.at[0], right)
    g_right = remote(ext_g.at[own], ext_g.at[low], ng_s.at[0], ng_r.at[0], right)
    k_left = remote(ext_k.at[own], ext_k.at[top], nk_s.at[1], nk_r.at[1], left)
    g_left = remote(ext_g.at[own], ext_g.at[top], ng_s.at[1], ng_r.at[1], left)

    @pl.when(box < n_box - 1)
    def _():
        g_right.start()
        k_right.start()

    @pl.when(box > 0)
    def _():
        g_left.start()
        k_left.start()

    @pl.when(box == 0)
    def _():
        ext_k[low] = jnp.zeros((nb, q, width), F32)
        ext_g[low] = jnp.zeros((nb, 8, width), F32)

    @pl.when(box == n_box - 1)
    def _():
        ext_k[top] = jnp.zeros((nb, q, width), F32)
        ext_g[top] = jnp.zeros((nb, 8, width), F32)

    poles = []
    for b in range(nb):
        lanes = slice(b * width, (b + 1) * width)
        poles.append(nt(b_ref[:, lanes], k_ref[:, lanes]))
    for h in range(nb // 2):
        fbuf[box, h * r : (h + 1) * r, :] = jnp.concatenate(
            [poles[2 * h], poles[2 * h + 1]], axis=1
        )

    cpole_own = nn(up_ref[...].T, jnp.concatenate(poles, axis=0))
    fine_rows = nb // 2 * r
    fbuf[box, fine_rows : fine_rows + r // 2, :] = jnp.concatenate(
        [cpole_own[: r // 2], cpole_own[r // 2 :]], axis=1
    )

    def spread(buf, s_sems, r_sems, fs_sems, fr_sems):
        mine = buf.at[box]
        copies = [remote(mine, mine, fs_sems.at[0], fr_sems.at[0], (leaf, sibling))]
        for d in range(1, nz):
            peer = 2 * lax.rem(z + d, nz) + core
            copies.append(remote(mine, mine, s_sems.at[d], r_sems.at[d], (leaf, peer)))
        return copies

    def forward(buf, fs_sems, fr_sems):
        result = []
        for d in range(1, nz):
            source = 2 * lax.rem(z + nz - d, nz) + core
            slot = buf.at[source]
            result.append(remote(slot, slot, fs_sems.at[d], fr_sems.at[d], (leaf, sibling)))
        return result

    fine_out = spread(fbuf, f_s, f_r, ff_s, ff_r)
    for copy in fine_out:
        copy.start()

    def to_split(i, carry):
        high, rest = split(ext_k[i])
        kcat[i] = jnp.concatenate([high, rest], axis=0)
        return carry

    lax.fori_loop(nb, 2 * nb, to_split, 0)
    lane4 = lax.broadcasted_iota(jnp.int32, (r, 4 * r), 1) // r
    for c in range(cf_ref.shape[0]):
        tfine[c] = jnp.concatenate([cf_ref[c]] * 4, axis=1)
    for c in range(cc_ref.shape[0]):
        tcoarse[c] = jnp.concatenate([cc_ref[c]] * 4, axis=1)

    @pl.when(box > 0)
    def _():
        g_right.wait_recv()

    @pl.when(box < n_box - 1)
    def _():
        g_left.wait_recv()

    shift = nb - first_box

    def source_box(b, e):
        return jnp.clip(near_ref[b, e] + shift, 0, 3 * nb - 1)

    pairs = near_count // 2

    def green_box(b, carry):
        target = geo_t[b]
        columns = [jnp.broadcast_to(target[:, c : c + 1], (width, width)) for c in range(4)]

        def pair(t, carry):
            for side in range(2):
                g = ext_g[source_box(b, 2 * t + side)]
                first = columns[0] - g[0:1]
                second = columns[1] - g[1:2]
                third = columns[2] - g[2:3]
                squared = first * first + second * second + third * third
                high, rest = split(lax.rsqrt(squared + columns[3] * g[3:4]))
                lanes = slice(side * width, (side + 1) * width)
                greens[b * pairs + t, :width, lanes] = high
                greens[b * pairs + t, width:, lanes] = rest
            return carry

        return lax.fori_loop(0, pairs, pair, carry)

    def near_box(b, carry):
        total = jnp.zeros((2 * q, 2 * width), F32)
        for t in range(pairs):
            source = jnp.concatenate(
                [kcat[source_box(b, 2 * t)], kcat[source_box(b, 2 * t + 1)]], axis=1
            )
            total = total + lax.dot_general(
                source, greens[b * pairs + t], (((1,), (1,)), ((), ())),
                preferred_element_type=F32,
            )
        half = total[:, :width] + total[:, width:]
        prod_ref[:, pl.ds(pl.multiple_of(b * width, width), width)] = half[:q] + half[q:]
        return carry

    fine_fwd = forward(fbuf, ff_s, ff_r)
    cuts = [nb * d // nz for d in range(nz + 1)]
    lax.fori_loop(0, cuts[1], green_box, 0)
    for d in range(1, nz):
        fine_out[d].wait_recv()
        fine_fwd[d - 1].start()
        if cuts[d + 1] > cuts[d]:
            lax.fori_loop(cuts[d], cuts[d + 1], green_box, 0)
    for copy in [fine_out[0]] + fine_fwd:
        copy.wait_recv()
    for i in range(n_box):
        lbuf[leaf, i] = fbuf[i, fine_rows : fine_rows + r // 2, :]
    leaf_out = [
        remote(
            lbuf.at[leaf], lbuf.at[leaf], cl_s.at[d], cl_r.at[d],
            (lax.rem(leaf + d, n_leaf), box),
        )
        for d in range(1, n_leaf)
    ]
    for copy in leaf_out:
        copy.start()

    @pl.when(box > 0)
    def _():
        k_right.wait_recv()

    @pl.when(box < n_box - 1)
    def _():
        k_left.wait_recv()

    lax.fori_loop(0, nb, to_split, 0)
    lax.fori_loop(2 * nb, 3 * nb, to_split, 0)
    lax.fori_loop(0, nb, near_box, 0)

    def open_fine(i, carry):
        for h in range(nb // 2):
            rows = fbuf[i, h * r : (h + 1) * r, :]
            fpole[i * nb + 2 * h] = rows[:, :q]
            fpole[i * nb + 2 * h + 1] = rows[:, q:]
        return carry

    lax.fori_loop(0, n_box, open_fine, 0)

    def open_coarse(i, carry):
        for h in range(n_leaf):
            rows = lbuf[h, i]
            cpole[h * n_box + i] = jnp.concatenate([rows[:, :q], rows[:, q:]], axis=0)
        return carry

    for copy in leaf_out:
        copy.wait_recv()
    lax.fori_loop(0, n_box, open_coarse, 0)

    def coupled(table, class_of, pole, index_of, live, entries):
        left_side = []
        for group in range(entries // 4):
            block = None
            for side in range(4):
                e = 4 * group + side
                mask = jnp.where(e < live, 1.0, 0.0).astype(F32)
                piece = table[class_of(e)] * mask
                block = piece if side == 0 else jnp.where(lane4 == side, piece, block)
            left_side.append(block)
        right_side = [pole[index_of(e)] for e in range(entries)]
        return nn(jnp.concatenate(left_side, axis=1), jnp.concatenate(right_side, axis=0))

    coarse_local = coupled(
        tcoarse, lambda e: cclass_ref[0, e], cpole, lambda e: clist_ref[0, e],
        ccount_ref[0], coarse_count,
    )
    lowered = nn(down_ref[...], coarse_local)
    for b in range(nb):
        dloc[b] = lowered[b * r : (b + 1) * r]

    def far_box(b, carry):
        local = dloc[b] + coupled(
            tfine, lambda e: fclass_ref[b, e], fpole,
            lambda e: jnp.clip(flist_ref[b, e] - group_first, 0, n_box * nb - 1),
            fcount_ref[b], far_count,
        )
        lanes = pl.ds(pl.multiple_of(b * width, width), width)
        prod_ref[:, lanes] = prod_ref[:, lanes] + nn(local.T, b_ref[:, lanes])
        return carry

    lax.fori_loop(0, nb, far_box, 0)

    stacked = jnp.concatenate([k_ref[...], prod_ref[...]], axis=0)
    gram = nt(stacked, stacked)
    share = rbuf.shape[1]
    for s in range(n_box):
        rbuf[s] = gram[s * share : (s + 1) * share]
    r_out = []
    for d in range(1, n_box):
        peer = lax.rem(box + d, n_box)
        r_out.append(
            remote(rbuf.at[peer], rrecv.at[box], r_s.at[d], r_r.at[d], (leaf, peer))
        )
        r_out[-1].start()
    rrecv[box] = rbuf[box]
    for copy in r_out:
        copy.wait_recv()
    part = rrecv[0]
    for s in range(1, n_box):
        part = part + rrecv[s]
    lrecv[leaf] = part
    l_out = []
    for d in range(1, n_leaf):
        peer = lax.rem(leaf + d, n_leaf)
        l_out.append(
            remote(lrecv.at[leaf], lrecv.at[leaf], l_s.at[d], l_r.at[d], (peer, box))
        )
        l_out[-1].start()
    for copy in l_out:
        copy.wait_recv()
    part = lrecv[0]
    for s in range(1, n_leaf):
        part = part + lrecv[s]
    gath[box] = part
    g_out = []
    for d in range(1, n_box):
        peer = lax.rem(box + d, n_box)
        g_out.append(remote(gath.at[box], gath.at[box], g_s.at[d], g_r.at[d], (leaf, peer)))
        g_out[-1].start()
    for copy in g_out:
        copy.wait_recv()
    red_ref[...] = gath[...]

    @pl.when(box < n_box - 1)
    def _():
        k_right.wait_send()
        g_right.wait_send()

    @pl.when(box > 0)
    def _():
        k_left.wait_send()
        g_left.wait_send()

    for copy in fine_out + fine_fwd + leaf_out + r_out + l_out + g_out:
        copy.wait_send()


def finish_kernel(panels, k_ref, prod_ref, red_ref, basis_ref, hess_ref, factor_ref):
    q = k_ref.shape[0]
    red = red_ref[...]
    basis_gram = red[:q, :q]
    mixed = red[:q, q:]
    mixed_t = red[q:, :q]
    image = red[q:, q:]
    inverse = 1.0 / panels
    hess = mixed * inverse
    hess_t = mixed_t * inverse
    hess_ref[...] = hess
    corrected = image - nn(mixed_t, hess) - nn(hess_t, mixed)
    corrected = (corrected + nn(nn(hess_t, basis_gram), hess)) * inverse
    eye = (
        lax.broadcasted_iota(jnp.int32, (q, q), 0) == lax.broadcasted_iota(jnp.int32, (q, q), 1)
    ).astype(F32)
    start = jnp.concatenate([corrected, eye], axis=1)
    tiles = [start[8 * t : 8 * t + 8] for t in range(q // 8)]
    row_id = lax.broadcasted_iota(jnp.int32, (8, 2 * q), 0)
    for p in range(q // 8):
        cols = [
            [jnp.broadcast_to(tiles[t][:, 8 * p + c : 8 * p + c + 1], (8, 2 * q)) for t in range(p, q // 8)]
            for c in range(8)
        ]
        for c in range(8):
            pivot = cols[c][0][c : c + 1]
            scale = lax.rsqrt(pivot)
            row = tiles[p][c : c + 1] * scale
            scaled = [tile * scale for tile in cols[c]]
            scaled[0] = jnp.where(row_id > c, scaled[0], 0.0)
            for j in range(c + 1, 8):
                value = cols[j][0][c : c + 1] * scale
                cols[j] = [x - s * value for x, s in zip(cols[j], scaled)]
            tiles[p] = jnp.where(row_id == c, row, tiles[p] - scaled[0] * row)
            for t in range(p + 1, q // 8):
                tiles[t] = tiles[t] - scaled[t - p] * row
    done = jnp.concatenate(tiles, axis=0)
    lower = done[:, :q].T
    keep = lax.broadcasted_iota(jnp.int32, (q, q), 0) >= lax.broadcasted_iota(jnp.int32, (q, q), 1)
    factor_ref[...] = jnp.where(keep, lower, 0.0)
    solve = jnp.where(keep, done[:, q:], 0.0)
    residual = prod_ref[...] - nn(hess_t, k_ref[...])
    basis_ref[...] = nn(solve, residual)


def per_device(
    krylov_block, bases, points, panel_size, panel_weight, near_list, far_list, far_class,
    far_count, coarse_list, coarse_class, coarse_count, couple_fine, couple_coarse,
    up_transfer, down_transfer,
):
    q, local = krylov_block.shape
    r = bases.shape[0]
    nb = near_list.shape[0]
    width = local // nb
    n_leaf = lax.axis_size("leaf")
    n_box = lax.axis_size("box")
    nz = n_box // 2
    share = 2 * q // n_box
    panels = local * n_leaf * n_box
    vmem = pl.BlockSpec(memory_space=pltpu.VMEM)
    smem = pl.BlockSpec(memory_space=pltpu.SMEM)
    dma = lambda n: pltpu.SemaphoreType.DMA((n,))
    product, reduced = pl.pallas_call(
        functools.partial(
            product_kernel, n_leaf, n_box, nb, width, float(width * near_list.shape[1])
        ),
        out_shape=(
            jax.ShapeDtypeStruct((q, local), F32),
            jax.ShapeDtypeStruct((n_box, share, 2 * q), F32),
        ),
        in_specs=[vmem] * 5 + [smem] * 7 + [vmem] * 4,
        out_specs=(vmem, vmem),
        scratch_shapes=[
            pltpu.VMEM((3 * nb, q, width), F32),
            pltpu.VMEM((3 * nb, 8, width), F32),
            pltpu.VMEM((3 * nb, 2 * q, width), BF16),
            pltpu.VMEM((nb, width, 8), F32),
            pltpu.VMEM((nb * (near_list.shape[1] // 2), 2 * width, 2 * width), BF16),
            pltpu.VMEM((n_box, nb // 2 * r + r // 2, 2 * q), F32),
            pltpu.VMEM((n_leaf, n_box, r // 2, 2 * q), F32),
            pltpu.VMEM((n_box * nb, r, q), F32),
            pltpu.VMEM((n_box * n_leaf, r, q), F32),
            pltpu.VMEM((couple_fine.shape[0], r, 4 * r), F32),
            pltpu.VMEM((couple_coarse.shape[0], r, 4 * r), F32),
            pltpu.VMEM((nb, r, q), F32),
            pltpu.VMEM((n_box, share, 2 * q), F32),
            pltpu.VMEM((n_box, share, 2 * q), F32),
            pltpu.VMEM((n_leaf, share, 2 * q), F32),
            pltpu.VMEM((n_box, share, 2 * q), F32),
            dma(2), dma(2), dma(2), dma(2),
            dma(nz), dma(nz), dma(nz), dma(nz),
            dma(n_leaf), dma(n_leaf),
            dma(n_box), dma(n_box), dma(n_leaf), dma(n_leaf), dma(n_box), dma(n_box),
        ],
        compiler_params=pltpu.CompilerParams(
            collective_id=0, has_side_effects=True, vmem_limit_bytes=63 * 2**20
        ),
    )(
        krylov_block, bases, points, panel_size[None, :], panel_weight[None, :],
        near_list, far_list, far_class, far_count, coarse_list, coarse_class, coarse_count,
        couple_fine, couple_coarse,
        up_transfer.reshape(-1, r), down_transfer.reshape(-1, r),
    )
    return pl.pallas_call(
        functools.partial(finish_kernel, float(panels)),
        out_shape=(
            jax.ShapeDtypeStruct((q, local), F32),
            jax.ShapeDtypeStruct((q, q), F32),
            jax.ShapeDtypeStruct((q, q), F32),
        ),
        in_specs=[vmem] * 3,
        out_specs=(vmem, vmem, vmem),
        compiler_params=pltpu.CompilerParams(vmem_limit_bytes=63 * 2**20),
    )(krylov_block, product, reduced.reshape(2 * q, 2 * q))


def solution(mesh):
    split_last = P(None, ("leaf", "box"))
    split_first = P(("leaf", "box"), None)
    flat = P(("leaf", "box"))
    in_specs = (
        split_last, split_last, split_last, flat, flat,
        split_first, split_first, split_first, flat,
        split_first, split_first, flat,
        P(), P(), P(), P(),
    )
    return jax.shard_map(
        per_device, mesh=mesh, in_specs=in_specs, out_specs=(split_last, P(), P()),
        check_vma=False,
    )
```

```python
import functools

import jax
import jax.numpy as jnp
from jax import lax
from jax.experimental import pallas as pl
from jax.experimental.pallas import tpu as pltpu
from jax.sharding import PartitionSpec as P

HIGHEST = lax.Precision.HIGHEST
MESH = pl.DeviceIdType.MESH
F32 = jnp.float32
BF16 = jnp.bfloat16


def nn(a, b):
    return jnp.dot(a, b, precision=HIGHEST, preferred_element_type=F32)


def nt(a, b):
    return lax.dot_general(
        a, b, (((1,), (1,)), ((), ())), precision=HIGHEST, preferred_element_type=F32
    )


def split(x):
    high = x.astype(BF16)
    return high, (x - high.astype(F32)).astype(BF16)


def product_kernel(
    n_leaf, n_box, nb, width, scale,
    k_ref, b_ref, pts_ref, size_ref, weight_ref,
    near_ref, flist_ref, fclass_ref, fcount_ref, clist_ref, cclass_ref, ccount_ref,
    cf_ref, cc_ref, up_ref, down_ref,
    prod_ref, red_ref,
    ext_k, ext_g, kcat, geo_t, greens, fbuf, lbuf, fpole, cpole, tfine, tcoarse, dloc,
    rbuf, rrecv, lrecv, gath,
    nk_s, nk_r, ng_s, ng_r, f_s, f_r, ff_s, ff_r, cl_s, cl_r,
    r_s, r_r, l_s, l_r, g_s, g_r,
):
    q = k_ref.shape[0]
    r = b_ref.shape[0]
    leaf = lax.axis_index("leaf")
    box = lax.axis_index("box")
    nz = n_box // 2
    core = lax.rem(box, 2)
    z = box // 2
    sibling = 2 * z + (1 - core)
    near_count = near_ref.shape[1]
    far_count = flist_ref.shape[1]
    coarse_count = clist_ref.shape[1]
    first_box = (leaf * n_box + box) * nb
    group_first = leaf * n_box * nb

    barrier = pltpu.get_barrier_semaphore()
    for d in range(1, n_box):
        pl.semaphore_signal(
            barrier, inc=1, device_id=(leaf, lax.rem(box + d, n_box)), device_id_type=MESH
        )
    for d in range(1, n_leaf):
        pl.semaphore_signal(
            barrier, inc=1, device_id=(lax.rem(leaf + d, n_leaf), box), device_id_type=MESH
        )

    def remote(src, dst, s_sem, r_sem, dev):
        return pltpu.make_async_remote_copy(
            src_ref=src, dst_ref=dst, send_sem=s_sem, recv_sem=r_sem,
            device_id=dev, device_id_type=MESH,
        )

    weights = weight_ref[...] * (1.0 / scale)
    weighted = k_ref[...] * weights
    geo = jnp.concatenate(
        [pts_ref[...], size_ref[...], weight_ref[...], pts_ref[...]], axis=0
    )
    for b in range(nb):
        lanes = slice(b * width, (b + 1) * width)
        ext_k[nb + b] = weighted[:, lanes]
        ext_g[nb + b] = geo[:, lanes]
        geo_t[b] = geo[:, lanes].T

    pl.semaphore_wait(barrier, n_box - 1 + n_leaf - 1)

    right = (leaf, lax.rem(box + 1, n_box))
    left = (leaf, lax.rem(box + n_box - 1, n_box))
    own = pl.ds(nb, nb)
    low = pl.ds(0, nb)
    top = pl.ds(2 * nb, nb)
    k_right = remote(ext_k.at[own], ext_k.at[low], nk_s.at[0], nk_r.at[0], right)
    g_right = remote(ext_g.at[own], ext_g.at[low], ng_s.at[0], ng_r.at[0], right)
    k_left = remote(ext_k.at[own], ext_k.at[top], nk_s.at[1], nk_r.at[1], left)
    g_left = remote(ext_g.at[own], ext_g.at[top], ng_s.at[1], ng_r.at[1], left)

    @pl.when(box < n_box - 1)
    def _():
        g_right.start()
        k_right.start()

    @pl.when(box > 0)
    def _():
        g_left.start()
        k_left.start()

    @pl.when(box == 0)
    def _():
        ext_k[low] = jnp.zeros((nb, q, width), F32)
        ext_g[low] = jnp.zeros((nb, 8, width), F32)

    @pl.when(box == n_box - 1)
    def _():
        ext_k[top] = jnp.zeros((nb, q, width), F32)
        ext_g[top] = jnp.zeros((nb, 8, width), F32)

    poles = []
    for b in range(nb):
        lanes = slice(b * width, (b + 1) * width)
        poles.append(nt(b_ref[:, lanes], k_ref[:, lanes]))
    for h in range(nb // 2):
        fbuf[box, h * r : (h + 1) * r, :] = jnp.concatenate(
            [poles[2 * h], poles[2 * h + 1]], axis=1
        )

    cpole_own = nn(up_ref[...].T, jnp.concatenate(poles, axis=0))
    fine_rows = nb // 2 * r
    fbuf[box, fine_rows : fine_rows + r // 2, :] = jnp.concatenate(
        [cpole_own[: r // 2], cpole_own[r // 2 :]], axis=1
    )

    def spread(buf, s_sems, r_sems, fs_sems, fr_sems):
        mine = buf.at[box]
        copies = [remote(mine, mine, fs_sems.at[0], fr_sems.at[0], (leaf, sibling))]
        for d in range(1, nz):
            peer = 2 * lax.rem(z + d, nz) + core
            copies.append(remote(mine, mine, s_sems.at[d], r_sems.at[d], (leaf, peer)))
        return copies

    def forward(buf, fs_sems, fr_sems):
        result = []
        for d in range(1, nz):
            source = 2 * lax.rem(z + nz - d, nz) + core
            slot = buf.at[source]
            result.append(remote(slot, slot, fs_sems.at[d], fr_sems.at[d], (leaf, sibling)))
        return result

    fine_out = spread(fbuf, f_s, f_r, ff_s, ff_r)
    for copy in fine_out:
        copy.start()

    def to_split(i, carry):
        high, rest = split(ext_k[i])
        kcat[i] = jnp.concatenate([high, rest], axis=0)
        return carry

    lax.fori_loop(nb, 2 * nb, to_split, 0, unroll=4)
    lane4 = lax.broadcasted_iota(jnp.int32, (r, 4 * r), 1) // r
    for c in range(cf_ref.shape[0]):
        tfine[c] = jnp.concatenate([cf_ref[c]] * 4, axis=1)
    for c in range(cc_ref.shape[0]):
        tcoarse[c] = jnp.concatenate([cc_ref[c]] * 4, axis=1)

    @pl.when(box > 0)
    def _():
        g_right.wait_recv()

    @pl.when(box < n_box - 1)
    def _():
        g_left.wait_recv()

    shift = nb - first_box

    def source_box(b, e):
        return jnp.clip(near_ref[b, e] + shift, 0, 3 * nb - 1)

    pairs = near_count // 2

    def green_box(b, carry):
        target = geo_t[b]
        columns = [jnp.broadcast_to(target[:, c : c + 1], (width, width)) for c in range(4)]

        def pair(t, carry):
            for side in range(2):
                g = ext_g[source_box(b, 2 * t + side)]
                first = columns[0] - g[0:1]
                second = columns[1] - g[1:2]
                third = columns[2] - g[2:3]
                squared = first * first + second * second + third * third
                high, rest = split(lax.rsqrt(squared + columns[3] * g[3:4]))
                lanes = slice(side * width, (side + 1) * width)
                greens[b * pairs + t, :width, lanes] = high
                greens[b * pairs + t, width:, lanes] = rest
            return carry

        return lax.fori_loop(0, pairs, pair, carry)

    def near_box(b, carry):
        total = jnp.zeros((2 * q, 2 * width), F32)
        for t in range(pairs):
            source = jnp.concatenate(
                [kcat[source_box(b, 2 * t)], kcat[source_box(b, 2 * t + 1)]], axis=1
            )
            total = total + lax.dot_general(
                source, greens[b * pairs + t], (((1,), (1,)), ((), ())),
                preferred_element_type=F32,
            )
        half = total[:, :width] + total[:, width:]
        prod_ref[:, pl.ds(pl.multiple_of(b * width, width), width)] = half[:q] + half[q:]
        return carry

    fine_fwd = forward(fbuf, ff_s, ff_r)
    cuts = [nb * d // nz for d in range(nz + 1)]
    lax.fori_loop(0, cuts[1], green_box, 0)
    for d in range(1, nz):
        fine_out[d].wait_recv()
        fine_fwd[d - 1].start()
        if cuts[d + 1] > cuts[d]:
            lax.fori_loop(cuts[d], cuts[d + 1], green_box, 0)
    for copy in [fine_out[0]] + fine_fwd:
        copy.wait_recv()
    for i in range(n_box):
        lbuf[leaf, i] = fbuf[i, fine_rows : fine_rows + r // 2, :]
    leaf_out = [
        remote(
            lbuf.at[leaf], lbuf.at[leaf], cl_s.at[d], cl_r.at[d],
            (lax.rem(leaf + d, n_leaf), box),
        )
        for d in range(1, n_leaf)
    ]
    for copy in leaf_out:
        copy.start()

    @pl.when(box > 0)
    def _():
        k_right.wait_recv()

    @pl.when(box < n_box - 1)
    def _():
        k_left.wait_recv()

    lax.fori_loop(0, nb, to_split, 0, unroll=4)
    lax.fori_loop(2 * nb, 3 * nb, to_split, 0, unroll=4)
    lax.fori_loop(0, nb, near_box, 0, unroll=2)

    def open_fine(i, carry):
        for h in range(nb // 2):
            rows = fbuf[i, h * r : (h + 1) * r, :]
            fpole[i * nb + 2 * h] = rows[:, :q]
            fpole[i * nb + 2 * h + 1] = rows[:, q:]
        return carry

    lax.fori_loop(0, n_box, open_fine, 0, unroll=2)

    def open_coarse(i, carry):
        for h in range(n_leaf):
            rows = lbuf[h, i]
            cpole[h * n_box + i] = jnp.concatenate([rows[:, :q], rows[:, q:]], axis=0)
        return carry

    for copy in leaf_out:
        copy.wait_recv()
    lax.fori_loop(0, n_box, open_coarse, 0, unroll=2)

    def coupled(table, class_of, pole, index_of, live, entries):
        left_side = []
        for group in range(entries // 4):
            block = None
            for side in range(4):
                e = 4 * group + side
                mask = jnp.where(e < live, 1.0, 0.0).astype(F32)
                piece = table[class_of(e)] * mask
                block = piece if side == 0 else jnp.where(lane4 == side, piece, block)
            left_side.append(block)
        right_side = [pole[index_of(e)] for e in range(entries)]
        return nn(jnp.concatenate(left_side, axis=1), jnp.concatenate(right_side, axis=0))

    coarse_local = coupled(
        tcoarse, lambda e: cclass_ref[0, e], cpole, lambda e: clist_ref[0, e],
        ccount_ref[0], coarse_count,
    )
    lowered = nn(down_ref[...], coarse_local)
    for b in range(nb):
        dloc[b] = lowered[b * r : (b + 1) * r]

    def far_box(b, carry):
        local = dloc[b] + coupled(
            tfine, lambda e: fclass_ref[b, e], fpole,
            lambda e: jnp.clip(flist_ref[b, e] - group_first, 0, n_box * nb - 1),
            fcount_ref[b], far_count,
        )
        lanes = pl.ds(pl.multiple_of(b * width, width), width)
        prod_ref[:, lanes] = prod_ref[:, lanes] + nn(local.T, b_ref[:, lanes])
        return carry

    lax.fori_loop(0, nb, far_box, 0, unroll=4)

    stacked = jnp.concatenate([k_ref[...], prod_ref[...]], axis=0)
    gram = nt(stacked, stacked)
    share = rbuf.shape[1]
    for s in range(n_box):
        rbuf[s] = gram[s * share : (s + 1) * share]
    r_out = []
    for d in range(1, n_box):
        peer = lax.rem(box + d, n_box)
        r_out.append(
            remote(rbuf.at[peer], rrecv.at[box], r_s.at[d], r_r.at[d], (leaf, peer))
        )
        r_out[-1].start()
    rrecv[box] = rbuf[box]
    for copy in r_out:
        copy.wait_recv()
    part = rrecv[0]
    for s in range(1, n_box):
        part = part + rrecv[s]
    lrecv[leaf] = part
    l_out = []
    for d in range(1, n_leaf):
        peer = lax.rem(leaf + d, n_leaf)
        l_out.append(
            remote(lrecv.at[leaf], lrecv.at[leaf], l_s.at[d], l_r.at[d], (peer, box))
        )
        l_out[-1].start()
    for copy in l_out:
        copy.wait_recv()
    part = lrecv[0]
    for s in range(1, n_leaf):
        part = part + lrecv[s]
    gath[box] = part
    g_out = []
    for d in range(1, n_box):
        peer = lax.rem(box + d, n_box)
        g_out.append(remote(gath.at[box], gath.at[box], g_s.at[d], g_r.at[d], (leaf, peer)))
        g_out[-1].start()
    for copy in g_out:
        copy.wait_recv()
    red_ref[...] = gath[...]

    @pl.when(box < n_box - 1)
    def _():
        k_right.wait_send()
        g_right.wait_send()

    @pl.when(box > 0)
    def _():
        k_left.wait_send()
        g_left.wait_send()

    for copy in fine_out + fine_fwd + leaf_out + r_out + l_out + g_out:
        copy.wait_send()


def finish_kernel(panels, k_ref, prod_ref, red_ref, basis_ref, hess_ref, factor_ref):
    q = k_ref.shape[0]
    red = red_ref[...]
    basis_gram = red[:q, :q]
    mixed = red[:q, q:]
    mixed_t = red[q:, :q]
    image = red[q:, q:]
    inverse = 1.0 / panels
    hess = mixed * inverse
    hess_t = mixed_t * inverse
    hess_ref[...] = hess
    corrected = image - nn(mixed_t, hess) - nn(hess_t, mixed)
    corrected = (corrected + nn(nn(hess_t, basis_gram), hess)) * inverse
    eye = (
        lax.broadcasted_iota(jnp.int32, (q, q), 0) == lax.broadcasted_iota(jnp.int32, (q, q), 1)
    ).astype(F32)
    start = jnp.concatenate([corrected, eye], axis=1)
    tiles = [start[8 * t : 8 * t + 8] for t in range(q // 8)]
    row_id = lax.broadcasted_iota(jnp.int32, (8, 2 * q), 0)
    for p in range(q // 8):
        cols = [
            [jnp.broadcast_to(tiles[t][:, 8 * p + c : 8 * p + c + 1], (8, 2 * q)) for t in range(p, q // 8)]
            for c in range(8)
        ]
        for c in range(8):
            pivot = cols[c][0][c : c + 1]
            scale = lax.rsqrt(pivot)
            row = tiles[p][c : c + 1] * scale
            scaled = [tile * scale for tile in cols[c]]
            scaled[0] = jnp.where(row_id > c, scaled[0], 0.0)
            for j in range(c + 1, 8):
                value = cols[j][0][c : c + 1] * scale
                cols[j] = [x - s * value for x, s in zip(cols[j], scaled)]
            tiles[p] = jnp.where(row_id == c, row, tiles[p] - scaled[0] * row)
            for t in range(p + 1, q // 8):
                tiles[t] = tiles[t] - scaled[t - p] * row
    done = jnp.concatenate(tiles, axis=0)
    lower = done[:, :q].T
    keep = lax.broadcasted_iota(jnp.int32, (q, q), 0) >= lax.broadcasted_iota(jnp.int32, (q, q), 1)
    factor_ref[...] = jnp.where(keep, lower, 0.0)
    solve = jnp.where(keep, done[:, q:], 0.0)
    residual = prod_ref[...] - nn(hess_t, k_ref[...])
    basis_ref[...] = nn(solve, residual)


def per_device(
    krylov_block, bases, points, panel_size, panel_weight, near_list, far_list, far_class,
    far_count, coarse_list, coarse_class, coarse_count, couple_fine, couple_coarse,
    up_transfer, down_transfer,
):
    q, local = krylov_block.shape
    r = bases.shape[0]
    nb = near_list.shape[0]
    width = local // nb
    n_leaf = lax.axis_size("leaf")
    n_box = lax.axis_size("box")
    nz = n_box // 2
    share = 2 * q // n_box
    panels = local * n_leaf * n_box
    vmem = pl.BlockSpec(memory_space=pltpu.VMEM)
    smem = pl.BlockSpec(memory_space=pltpu.SMEM)
    dma = lambda n: pltpu.SemaphoreType.DMA((n,))
    product, reduced = pl.pallas_call(
        functools.partial(
            product_kernel, n_leaf, n_box, nb, width, float(width * near_list.shape[1])
        ),
        out_shape=(
            jax.ShapeDtypeStruct((q, local), F32),
            jax.ShapeDtypeStruct((n_box, share, 2 * q), F32),
        ),
        in_specs=[vmem] * 5 + [smem] * 7 + [vmem] * 4,
        out_specs=(vmem, vmem),
        scratch_shapes=[
            pltpu.VMEM((3 * nb, q, width), F32),
            pltpu.VMEM((3 * nb, 8, width), F32),
            pltpu.VMEM((3 * nb, 2 * q, width), BF16),
            pltpu.VMEM((nb, width, 8), F32),
            pltpu.VMEM((nb * (near_list.shape[1] // 2), 2 * width, 2 * width), BF16),
            pltpu.VMEM((n_box, nb // 2 * r + r // 2, 2 * q), F32),
            pltpu.VMEM((n_leaf, n_box, r // 2, 2 * q), F32),
            pltpu.VMEM((n_box * nb, r, q), F32),
            pltpu.VMEM((n_box * n_leaf, r, q), F32),
            pltpu.VMEM((couple_fine.shape[0], r, 4 * r), F32),
            pltpu.VMEM((couple_coarse.shape[0], r, 4 * r), F32),
            pltpu.VMEM((nb, r, q), F32),
            pltpu.VMEM((n_box, share, 2 * q), F32),
            pltpu.VMEM((n_box, share, 2 * q), F32),
            pltpu.VMEM((n_leaf, share, 2 * q), F32),
            pltpu.VMEM((n_box, share, 2 * q), F32),
            dma(2), dma(2), dma(2), dma(2),
            dma(nz), dma(nz), dma(nz), dma(nz),
            dma(n_leaf), dma(n_leaf),
            dma(n_box), dma(n_box), dma(n_leaf), dma(n_leaf), dma(n_box), dma(n_box),
        ],
        compiler_params=pltpu.CompilerParams(
            collective_id=0, has_side_effects=True, vmem_limit_bytes=63 * 2**20
        ),
    )(
        krylov_block, bases, points, panel_size[None, :], panel_weight[None, :],
        near_list, far_list, far_class, far_count, coarse_list, coarse_class, coarse_count,
        couple_fine, couple_coarse,
        up_transfer.reshape(-1, r), down_transfer.reshape(-1, r),
    )
    return pl.pallas_call(
        functools.partial(finish_kernel, float(panels)),
        out_shape=(
            jax.ShapeDtypeStruct((q, local), F32),
            jax.ShapeDtypeStruct((q, q), F32),
            jax.ShapeDtypeStruct((q, q), F32),
        ),
        in_specs=[vmem] * 3,
        out_specs=(vmem, vmem, vmem),
        compiler_params=pltpu.CompilerParams(vmem_limit_bytes=63 * 2**20),
    )(krylov_block, product, reduced.reshape(2 * q, 2 * q))


def solution(mesh):
    split_last = P(None, ("leaf", "box"))
    split_first = P(("leaf", "box"), None)
    flat = P(("leaf", "box"))
    in_specs = (
        split_last, split_last, split_last, flat, flat,
        split_first, split_first, split_first, flat,
        split_first, split_first, flat,
        P(), P(), P(), P(),
    )
    return jax.shard_map(
        per_device, mesh=mesh, in_specs=in_specs, out_specs=(split_last, P(), P()),
        check_vma=False,
    )
```

```python
import functools

import jax
import jax.numpy as jnp
from jax import lax
from jax.experimental import pallas as pl
from jax.experimental.pallas import tpu as pltpu
from jax.sharding import PartitionSpec as P

HIGHEST = lax.Precision.HIGHEST
MESH = pl.DeviceIdType.MESH
F32 = jnp.float32
BF16 = jnp.bfloat16


def nn(a, b):
    return jnp.dot(a, b, precision=HIGHEST, preferred_element_type=F32)


def nt(a, b):
    return lax.dot_general(
        a, b, (((1,), (1,)), ((), ())), precision=HIGHEST, preferred_element_type=F32
    )


def split(x):
    high = x.astype(BF16)
    return high, (x - high.astype(F32)).astype(BF16)


def product_kernel(
    n_leaf, n_box, nb, width, scale,
    k_ref, b_ref, pts_ref, size_ref, weight_ref,
    near_ref, flist_ref, fclass_ref, fcount_ref, clist_ref, cclass_ref, ccount_ref,
    cf_ref, cc_ref, up_ref, down_ref,
    prod_ref, red_ref, own_ref,
    ext_k, ext_g, kcat, geo_t, greens, fbuf, lbuf, fpole, cpole, tfine, tcoarse, dloc,
    rbuf, rrecv, lrecv, gath,
    nk_s, nk_r, ng_s, ng_r, f_s, f_r, ff_s, ff_r, cl_s, cl_r,
    r_s, r_r, l_s, l_r, g_s, g_r,
):
    q = k_ref.shape[0]
    r = b_ref.shape[0]
    leaf = lax.axis_index("leaf")
    box = lax.axis_index("box")
    nz = n_box // 2
    core = lax.rem(box, 2)
    z = box // 2
    sibling = 2 * z + (1 - core)
    near_count = near_ref.shape[1]
    far_count = flist_ref.shape[1]
    coarse_count = clist_ref.shape[1]
    first_box = (leaf * n_box + box) * nb
    group_first = leaf * n_box * nb

    barrier = pltpu.get_barrier_semaphore()
    for d in range(1, n_box):
        pl.semaphore_signal(
            barrier, inc=1, device_id=(leaf, lax.rem(box + d, n_box)), device_id_type=MESH
        )
    for d in range(1, n_leaf):
        pl.semaphore_signal(
            barrier, inc=1, device_id=(lax.rem(leaf + d, n_leaf), box), device_id_type=MESH
        )

    def remote(src, dst, s_sem, r_sem, dev):
        return pltpu.make_async_remote_copy(
            src_ref=src, dst_ref=dst, send_sem=s_sem, recv_sem=r_sem,
            device_id=dev, device_id_type=MESH,
        )

    weights = weight_ref[...] * (1.0 / scale)
    weighted = k_ref[...] * weights
    geo = jnp.concatenate(
        [pts_ref[...], size_ref[...], weight_ref[...], pts_ref[...]], axis=0
    )
    for b in range(nb):
        lanes = slice(b * width, (b + 1) * width)
        ext_k[nb + b] = weighted[:, lanes]
        ext_g[nb + b] = geo[:, lanes]
        geo_t[b] = geo[:, lanes].T

    pl.semaphore_wait(barrier, n_box - 1 + n_leaf - 1)

    right = (leaf, lax.rem(box + 1, n_box))
    left = (leaf, lax.rem(box + n_box - 1, n_box))
    own = pl.ds(nb, nb)
    low = pl.ds(0, nb)
    top = pl.ds(2 * nb, nb)
    k_right = remote(ext_k.at[own], ext_k.at[low], nk_s.at[0], nk_r.at[0], right)
    g_right = remote(ext_g.at[own], ext_g.at[low], ng_s.at[0], ng_r.at[0], right)
    k_left = remote(ext_k.at[own], ext_k.at[top], nk_s.at[1], nk_r.at[1], left)
    g_left = remote(ext_g.at[own], ext_g.at[top], ng_s.at[1], ng_r.at[1], left)

    @pl.when(box < n_box - 1)
    def _():
        g_right.start()
        k_right.start()

    @pl.when(box > 0)
    def _():
        g_left.start()
        k_left.start()

    @pl.when(box == 0)
    def _():
        ext_k[low] = jnp.zeros((nb, q, width), F32)
        ext_g[low] = jnp.zeros((nb, 8, width), F32)

    @pl.when(box == n_box - 1)
    def _():
        ext_k[top] = jnp.zeros((nb, q, width), F32)
        ext_g[top] = jnp.zeros((nb, 8, width), F32)

    poles = []
    for b in range(nb):
        lanes = slice(b * width, (b + 1) * width)
        poles.append(nt(b_ref[:, lanes], k_ref[:, lanes]))
    for h in range(nb // 2):
        fbuf[box, h * r : (h + 1) * r, :] = jnp.concatenate(
            [poles[2 * h], poles[2 * h + 1]], axis=1
        )

    cpole_own = nn(up_ref[...].T, jnp.concatenate(poles, axis=0))
    fine_rows = nb // 2 * r
    fbuf[box, fine_rows : fine_rows + r // 2, :] = jnp.concatenate(
        [cpole_own[: r // 2], cpole_own[r // 2 :]], axis=1
    )
    own_gram = nt(k_ref[...], k_ref[...])
    own_first = fine_rows + r // 2
    fbuf[box, own_first : own_first + q // 2, :] = jnp.concatenate(
        [own_gram[: q // 2], own_gram[q // 2 :]], axis=1
    )

    def spread(buf, s_sems, r_sems, fs_sems, fr_sems):
        mine = buf.at[box]
        copies = [remote(mine, mine, fs_sems.at[0], fr_sems.at[0], (leaf, sibling))]
        for d in range(1, nz):
            peer = 2 * lax.rem(z + d, nz) + core
            copies.append(remote(mine, mine, s_sems.at[d], r_sems.at[d], (leaf, peer)))
        return copies

    def forward(buf, fs_sems, fr_sems):
        result = []
        for d in range(1, nz):
            source = 2 * lax.rem(z + nz - d, nz) + core
            slot = buf.at[source]
            result.append(remote(slot, slot, fs_sems.at[d], fr_sems.at[d], (leaf, sibling)))
        return result

    fine_out = spread(fbuf, f_s, f_r, ff_s, ff_r)
    for copy in fine_out:
        copy.start()

    def to_split(i, carry):
        high, rest = split(ext_k[i])
        kcat[i] = jnp.concatenate([high, rest], axis=0)
        return carry

    lax.fori_loop(nb, 2 * nb, to_split, 0, unroll=4)
    lane4 = lax.broadcasted_iota(jnp.int32, (r, 4 * r), 1) // r
    for c in range(cf_ref.shape[0]):
        tfine[c] = jnp.concatenate([cf_ref[c]] * 4, axis=1)
    for c in range(cc_ref.shape[0]):
        tcoarse[c] = jnp.concatenate([cc_ref[c]] * 4, axis=1)

    @pl.when(box > 0)
    def _():
        g_right.wait_recv()

    @pl.when(box < n_box - 1)
    def _():
        g_left.wait_recv()

    shift = nb - first_box

    def source_box(b, e):
        return jnp.clip(near_ref[b, e] + shift, 0, 3 * nb - 1)

    pairs = near_count // 2

    def green_box(b, carry):
        target = geo_t[b]
        columns = [jnp.broadcast_to(target[:, c : c + 1], (width, width)) for c in range(4)]

        def pair(t, carry):
            for side in range(2):
                g = ext_g[source_box(b, 2 * t + side)]
                first = columns[0] - g[0:1]
                second = columns[1] - g[1:2]
                third = columns[2] - g[2:3]
                squared = first * first + second * second + third * third
                high, rest = split(lax.rsqrt(squared + columns[3] * g[3:4]))
                lanes = slice(side * width, (side + 1) * width)
                greens[b * pairs + t, :width, lanes] = high
                greens[b * pairs + t, width:, lanes] = rest
            return carry

        return lax.fori_loop(0, pairs, pair, carry)

    def near_box(b, carry):
        total = jnp.zeros((2 * q, 2 * width), F32)
        for t in range(pairs):
            source = jnp.concatenate(
                [kcat[source_box(b, 2 * t)], kcat[source_box(b, 2 * t + 1)]], axis=1
            )
            total = total + lax.dot_general(
                source, greens[b * pairs + t], (((1,), (1,)), ((), ())),
                preferred_element_type=F32,
            )
        half = total[:, :width] + total[:, width:]
        prod_ref[:, pl.ds(pl.multiple_of(b * width, width), width)] = half[:q] + half[q:]
        return carry

    fine_fwd = forward(fbuf, ff_s, ff_r)
    cuts = [nb * d // nz for d in range(nz + 1)]
    lax.fori_loop(0, cuts[1], green_box, 0)
    for d in range(1, nz):
        fine_out[d].wait_recv()
        fine_fwd[d - 1].start()
        if cuts[d + 1] > cuts[d]:
            lax.fori_loop(cuts[d], cuts[d + 1], green_box, 0)
    for copy in [fine_out[0]] + fine_fwd:
        copy.wait_recv()
    for i in range(n_box):
        lbuf[leaf, i] = fbuf[i, fine_rows : fine_rows + r // 2, :]
    own_sum = fbuf[0, own_first : own_first + q // 2, :]
    for i in range(1, n_box):
        own_sum = own_sum + fbuf[i, own_first : own_first + q // 2, :]
    for i in range(q // r):
        lbuf[leaf, n_box + i] = own_sum[i * (r // 2) : (i + 1) * (r // 2)]
    leaf_out = [
        remote(
            lbuf.at[leaf], lbuf.at[leaf], cl_s.at[d], cl_r.at[d],
            (lax.rem(leaf + d, n_leaf), box),
        )
        for d in range(1, n_leaf)
    ]
    for copy in leaf_out:
        copy.start()

    @pl.when(box > 0)
    def _():
        k_right.wait_recv()

    @pl.when(box < n_box - 1)
    def _():
        k_left.wait_recv()

    lax.fori_loop(0, nb, to_split, 0, unroll=4)
    lax.fori_loop(2 * nb, 3 * nb, to_split, 0, unroll=4)
    lax.fori_loop(0, nb, near_box, 0, unroll=2)

    def open_fine(i, carry):
        for h in range(nb // 2):
            rows = fbuf[i, h * r : (h + 1) * r, :]
            fpole[i * nb + 2 * h] = rows[:, :q]
            fpole[i * nb + 2 * h + 1] = rows[:, q:]
        return carry

    lax.fori_loop(0, n_box, open_fine, 0, unroll=2)

    def open_coarse(i, carry):
        for h in range(n_leaf):
            rows = lbuf[h, i]
            cpole[h * n_box + i] = jnp.concatenate([rows[:, :q], rows[:, q:]], axis=0)
        return carry

    for copy in leaf_out:
        copy.wait_recv()
    lax.fori_loop(0, n_box, open_coarse, 0, unroll=2)
    for i in range(q // r):
        own_sum = lbuf[0, n_box + i]
        for h in range(1, n_leaf):
            own_sum = own_sum + lbuf[h, n_box + i]
        own_ref[i * (r // 2) : (i + 1) * (r // 2), :] = own_sum

    def coupled(table, class_of, pole, index_of, live, entries):
        left_side = []
        for group in range(entries // 4):
            block = None
            for side in range(4):
                e = 4 * group + side
                mask = jnp.where(e < live, 1.0, 0.0).astype(F32)
                piece = table[class_of(e)] * mask
                block = piece if side == 0 else jnp.where(lane4 == side, piece, block)
            left_side.append(block)
        right_side = [pole[index_of(e)] for e in range(entries)]
        return nn(jnp.concatenate(left_side, axis=1), jnp.concatenate(right_side, axis=0))

    coarse_local = coupled(
        tcoarse, lambda e: cclass_ref[0, e], cpole, lambda e: clist_ref[0, e],
        ccount_ref[0], coarse_count,
    )
    lowered = nn(down_ref[...], coarse_local)
    for b in range(nb):
        dloc[b] = lowered[b * r : (b + 1) * r]

    def far_box(b, carry):
        local = dloc[b] + coupled(
            tfine, lambda e: fclass_ref[b, e], fpole,
            lambda e: jnp.clip(flist_ref[b, e] - group_first, 0, n_box * nb - 1),
            fcount_ref[b], far_count,
        )
        lanes = pl.ds(pl.multiple_of(b * width, width), width)
        prod_ref[:, lanes] = prod_ref[:, lanes] + nn(local.T, b_ref[:, lanes])
        return carry

    lax.fori_loop(0, nb, far_box, 0, unroll=4)

    stacked = jnp.concatenate([k_ref[...], prod_ref[...]], axis=0)
    gram = nt(stacked, prod_ref[...])
    gram = jnp.concatenate([gram[:q], gram[q:]], axis=1)
    share = rbuf.shape[1]
    for s in range(n_box):
        rbuf[s] = gram[s * share : (s + 1) * share]
    r_out = []
    for d in range(1, n_box):
        peer = lax.rem(box + d, n_box)
        r_out.append(
            remote(rbuf.at[peer], rrecv.at[box], r_s.at[d], r_r.at[d], (leaf, peer))
        )
        r_out[-1].start()
    rrecv[box] = rbuf[box]
    for copy in r_out:
        copy.wait_recv()
    part = rrecv[0]
    for s in range(1, n_box):
        part = part + rrecv[s]
    lrecv[leaf] = part
    l_out = []
    for d in range(1, n_leaf):
        peer = lax.rem(leaf + d, n_leaf)
        l_out.append(
            remote(lrecv.at[leaf], lrecv.at[leaf], l_s.at[d], l_r.at[d], (peer, box))
        )
        l_out[-1].start()
    for copy in l_out:
        copy.wait_recv()
    part = lrecv[0]
    for s in range(1, n_leaf):
        part = part + lrecv[s]
    gath[box] = part
    g_out = []
    for d in range(1, n_box):
        peer = lax.rem(box + d, n_box)
        g_out.append(remote(gath.at[box], gath.at[box], g_s.at[d], g_r.at[d], (leaf, peer)))
        g_out[-1].start()
    for copy in g_out:
        copy.wait_recv()
    red_ref[...] = gath[...]

    @pl.when(box < n_box - 1)
    def _():
        k_right.wait_send()
        g_right.wait_send()

    @pl.when(box > 0)
    def _():
        k_left.wait_send()
        g_left.wait_send()

    for copy in fine_out + fine_fwd + leaf_out + r_out + l_out + g_out:
        copy.wait_send()


def finish_kernel(panels, k_ref, prod_ref, red_ref, own_ref, basis_ref, hess_ref, factor_ref):
    q = k_ref.shape[0]
    red = red_ref[...]
    own = own_ref[...]
    basis_gram = jnp.concatenate([own[:, :q], own[:, q:]], axis=0)
    mixed = red[:, :q]
    mixed_t = mixed.T
    image = red[:, q:]
    inverse = 1.0 / panels
    hess = mixed * inverse
    hess_t = mixed_t * inverse
    hess_ref[...] = hess
    corrected = image - nn(mixed_t, hess) - nn(hess_t, mixed)
    corrected = (corrected + nn(nn(hess_t, basis_gram), hess)) * inverse
    eye = (
        lax.broadcasted_iota(jnp.int32, (q, q), 0) == lax.broadcasted_iota(jnp.int32, (q, q), 1)
    ).astype(F32)
    start = jnp.concatenate([corrected, eye], axis=1)
    tiles = [start[8 * t : 8 * t + 8] for t in range(q // 8)]
    row_id = lax.broadcasted_iota(jnp.int32, (8, 2 * q), 0)
    for p in range(q // 8):
        cols = [
            [jnp.broadcast_to(tiles[t][:, 8 * p + c : 8 * p + c + 1], (8, 2 * q)) for t in range(p, q // 8)]
            for c in range(8)
        ]
        for c in range(8):
            pivot = cols[c][0][c : c + 1]
            scale = lax.rsqrt(pivot)
            row = tiles[p][c : c + 1] * scale
            scaled = [tile * scale for tile in cols[c]]
            scaled[0] = jnp.where(row_id > c, scaled[0], 0.0)
            for j in range(c + 1, 8):
                value = cols[j][0][c : c + 1] * scale
                cols[j] = [x - s * value for x, s in zip(cols[j], scaled)]
            tiles[p] = jnp.where(row_id == c, row, tiles[p] - scaled[0] * row)
            for t in range(p + 1, q // 8):
                tiles[t] = tiles[t] - scaled[t - p] * row
    done = jnp.concatenate(tiles, axis=0)
    lower = done[:, :q].T
    keep = lax.broadcasted_iota(jnp.int32, (q, q), 0) >= lax.broadcasted_iota(jnp.int32, (q, q), 1)
    factor_ref[...] = jnp.where(keep, lower, 0.0)
    solve = jnp.where(keep, done[:, q:], 0.0)
    residual = prod_ref[...] - nn(hess_t, k_ref[...])
    basis_ref[...] = nn(solve, residual)


def per_device(
    krylov_block, bases, points, panel_size, panel_weight, near_list, far_list, far_class,
    far_count, coarse_list, coarse_class, coarse_count, couple_fine, couple_coarse,
    up_transfer, down_transfer,
):
    q, local = krylov_block.shape
    r = bases.shape[0]
    nb = near_list.shape[0]
    width = local // nb
    n_leaf = lax.axis_size("leaf")
    n_box = lax.axis_size("box")
    nz = n_box // 2
    share = q // n_box
    panels = local * n_leaf * n_box
    vmem = pl.BlockSpec(memory_space=pltpu.VMEM)
    smem = pl.BlockSpec(memory_space=pltpu.SMEM)
    dma = lambda n: pltpu.SemaphoreType.DMA((n,))
    product, reduced, own_gram = pl.pallas_call(
        functools.partial(
            product_kernel, n_leaf, n_box, nb, width, float(width * near_list.shape[1])
        ),
        out_shape=(
            jax.ShapeDtypeStruct((q, local), F32),
            jax.ShapeDtypeStruct((n_box, share, 2 * q), F32),
            jax.ShapeDtypeStruct((q // 2, 2 * q), F32),
        ),
        in_specs=[vmem] * 5 + [smem] * 7 + [vmem] * 4,
        out_specs=(vmem, vmem, vmem),
        scratch_shapes=[
            pltpu.VMEM((3 * nb, q, width), F32),
            pltpu.VMEM((3 * nb, 8, width), F32),
            pltpu.VMEM((3 * nb, 2 * q, width), BF16),
            pltpu.VMEM((nb, width, 8), F32),
            pltpu.VMEM((nb * (near_list.shape[1] // 2), 2 * width, 2 * width), BF16),
            pltpu.VMEM((n_box, nb // 2 * r + r // 2 + q // 2, 2 * q), F32),
            pltpu.VMEM((n_leaf, n_box + q // r, r // 2, 2 * q), F32),
            pltpu.VMEM((n_box * nb, r, q), F32),
            pltpu.VMEM((n_box * n_leaf, r, q), F32),
            pltpu.VMEM((couple_fine.shape[0], r, 4 * r), F32),
            pltpu.VMEM((couple_coarse.shape[0], r, 4 * r), F32),
            pltpu.VMEM((nb, r, q), F32),
            pltpu.VMEM((n_box, share, 2 * q), F32),
            pltpu.VMEM((n_box, share, 2 * q), F32),
            pltpu.VMEM((n_leaf, share, 2 * q), F32),
            pltpu.VMEM((n_box, share, 2 * q), F32),
            dma(2), dma(2), dma(2), dma(2),
            dma(nz), dma(nz), dma(nz), dma(nz),
            dma(n_leaf), dma(n_leaf),
            dma(n_box), dma(n_box), dma(n_leaf), dma(n_leaf), dma(n_box), dma(n_box),
        ],
        compiler_params=pltpu.CompilerParams(
            collective_id=0, has_side_effects=True, vmem_limit_bytes=63 * 2**20
        ),
    )(
        krylov_block, bases, points, panel_size[None, :], panel_weight[None, :],
        near_list, far_list, far_class, far_count, coarse_list, coarse_class, coarse_count,
        couple_fine, couple_coarse,
        up_transfer.reshape(-1, r), down_transfer.reshape(-1, r),
    )
    return pl.pallas_call(
        functools.partial(finish_kernel, float(panels)),
        out_shape=(
            jax.ShapeDtypeStruct((q, local), F32),
            jax.ShapeDtypeStruct((q, q), F32),
            jax.ShapeDtypeStruct((q, q), F32),
        ),
        in_specs=[vmem] * 4,
        out_specs=(vmem, vmem, vmem),
        compiler_params=pltpu.CompilerParams(vmem_limit_bytes=63 * 2**20),
    )(krylov_block, product, reduced.reshape(q, 2 * q), own_gram)


def solution(mesh):
    split_last = P(None, ("leaf", "box"))
    split_first = P(("leaf", "box"), None)
    flat = P(("leaf", "box"))
    in_specs = (
        split_last, split_last, split_last, flat, flat,
        split_first, split_first, split_first, flat,
        split_first, split_first, flat,
        P(), P(), P(), P(),
    )
    return jax.shard_map(
        per_device, mesh=mesh, in_specs=in_specs, out_specs=(split_last, P(), P()),
        check_vma=False,
    )
```

```python
import functools

import jax
import jax.numpy as jnp
from jax import lax
from jax.experimental import pallas as pl
from jax.experimental.pallas import tpu as pltpu
from jax.sharding import PartitionSpec as P

HIGHEST = lax.Precision.HIGHEST
MESH = pl.DeviceIdType.MESH
F32 = jnp.float32
BF16 = jnp.bfloat16


def nn(a, b):
    return jnp.dot(a, b, precision=HIGHEST, preferred_element_type=F32)


def nt(a, b):
    return lax.dot_general(
        a, b, (((1,), (1,)), ((), ())), precision=HIGHEST, preferred_element_type=F32
    )


def split(x):
    high = x.astype(BF16)
    return high, (x - high.astype(F32)).astype(BF16)


def product_kernel(
    n_leaf, n_box, nb, width, scale,
    k_ref, b_ref, pts_ref, size_ref, weight_ref,
    near_ref, flist_ref, fclass_ref, fcount_ref, clist_ref, cclass_ref, ccount_ref,
    cf_ref, cc_ref, up_ref, down_ref,
    prod_ref, red_ref,
    ext_k, ext_g, kcat, geo_t, greens, fbuf, lbuf, fpole, cpole, tfine, tcoarse, dloc,
    rbuf, rrecv, lrecv, gath,
    nk_s, nk_r, ng_s, ng_r, f_s, f_r, ff_s, ff_r, cl_s, cl_r,
    r_s, r_r, l_s, l_r, g_s, g_r,
):
    q = k_ref.shape[0]
    r = b_ref.shape[0]
    leaf = lax.axis_index("leaf")
    box = lax.axis_index("box")
    nz = n_box // 2
    core = lax.rem(box, 2)
    z = box // 2
    sibling = 2 * z + (1 - core)
    near_count = near_ref.shape[1]
    far_count = flist_ref.shape[1]
    coarse_count = clist_ref.shape[1]
    first_box = (leaf * n_box + box) * nb
    group_first = leaf * n_box * nb

    barrier = pltpu.get_barrier_semaphore()
    for d in range(1, n_box):
        pl.semaphore_signal(
            barrier, inc=1, device_id=(leaf, lax.rem(box + d, n_box)), device_id_type=MESH
        )
    for d in range(1, n_leaf):
        pl.semaphore_signal(
            barrier, inc=1, device_id=(lax.rem(leaf + d, n_leaf), box), device_id_type=MESH
        )

    def remote(src, dst, s_sem, r_sem, dev):
        return pltpu.make_async_remote_copy(
            src_ref=src, dst_ref=dst, send_sem=s_sem, recv_sem=r_sem,
            device_id=dev, device_id_type=MESH,
        )

    weights = weight_ref[...] * (1.0 / scale)
    weighted = k_ref[...] * weights
    geo = jnp.concatenate(
        [pts_ref[...], size_ref[...], weight_ref[...], pts_ref[...]], axis=0
    )
    for b in range(nb):
        lanes = slice(b * width, (b + 1) * width)
        ext_k[nb + b] = weighted[:, lanes]
        ext_g[nb + b] = geo[:, lanes]
        geo_t[b] = geo[:, lanes].T

    pl.semaphore_wait(barrier, n_box - 1 + n_leaf - 1)

    right = (leaf, lax.rem(box + 1, n_box))
    left = (leaf, lax.rem(box + n_box - 1, n_box))
    own = pl.ds(nb, nb)
    low = pl.ds(0, nb)
    top = pl.ds(2 * nb, nb)
    k_right = remote(ext_k.at[own], ext_k.at[low], nk_s.at[0], nk_r.at[0], right)
    g_right = remote(ext_g.at[own], ext_g.at[low], ng_s.at[0], ng_r.at[0], right)
    k_left = remote(ext_k.at[own], ext_k.at[top], nk_s.at[1], nk_r.at[1], left)
    g_left = remote(ext_g.at[own], ext_g.at[top], ng_s.at[1], ng_r.at[1], left)

    @pl.when(box < n_box - 1)
    def _():
        g_right.start()
        k_right.start()

    @pl.when(box > 0)
    def _():
        g_left.start()
        k_left.start()

    @pl.when(box == 0)
    def _():
        ext_k[low] = jnp.zeros((nb, q, width), F32)
        ext_g[low] = jnp.zeros((nb, 8, width), F32)

    @pl.when(box == n_box - 1)
    def _():
        ext_k[top] = jnp.zeros((nb, q, width), F32)
        ext_g[top] = jnp.zeros((nb, 8, width), F32)

    poles = []
    for b in range(nb):
        lanes = slice(b * width, (b + 1) * width)
        poles.append(nt(b_ref[:, lanes], k_ref[:, lanes]))
    for h in range(nb // 2):
        fbuf[box, h * r : (h + 1) * r, :] = jnp.concatenate(
            [poles[2 * h], poles[2 * h + 1]], axis=1
        )

    cpole_own = nn(up_ref[...].T, jnp.concatenate(poles, axis=0))
    fine_rows = nb // 2 * r
    fbuf[box, fine_rows : fine_rows + r // 2, :] = jnp.concatenate(
        [cpole_own[: r // 2], cpole_own[r // 2 :]], axis=1
    )

    def spread(buf, s_sems, r_sems, fs_sems, fr_sems):
        mine = buf.at[box]
        copies = [remote(mine, mine, fs_sems.at[0], fr_sems.at[0], (leaf, sibling))]
        for d in range(1, nz):
            peer = 2 * lax.rem(z + d, nz) + core
            copies.append(remote(mine, mine, s_sems.at[d], r_sems.at[d], (leaf, peer)))
        return copies

    def forward(buf, fs_sems, fr_sems):
        result = []
        for d in range(1, nz):
            source = 2 * lax.rem(z + nz - d, nz) + core
            slot = buf.at[source]
            result.append(remote(slot, slot, fs_sems.at[d], fr_sems.at[d], (leaf, sibling)))
        return result

    fine_out = spread(fbuf, f_s, f_r, ff_s, ff_r)
    for copy in fine_out:
        copy.start()

    def to_split(i, carry):
        high, rest = split(ext_k[i])
        kcat[i] = jnp.concatenate([high, rest], axis=0)
        return carry

    lax.fori_loop(nb, 2 * nb, to_split, 0, unroll=4)
    lane4 = lax.broadcasted_iota(jnp.int32, (r, 4 * r), 1) // r
    for c in range(cf_ref.shape[0]):
        tfine[c] = jnp.concatenate([cf_ref[c]] * 4, axis=1)
    for c in range(cc_ref.shape[0]):
        tcoarse[c] = jnp.concatenate([cc_ref[c]] * 4, axis=1)

    @pl.when(box > 0)
    def _():
        g_right.wait_recv()

    @pl.when(box < n_box - 1)
    def _():
        g_left.wait_recv()

    shift = nb - first_box

    def source_box(b, e):
        return jnp.clip(near_ref[b, e] + shift, 0, 3 * nb - 1)

    pairs = near_count // 2

    def green_box(b, carry):
        target = geo_t[b]
        columns = [jnp.broadcast_to(target[:, c : c + 1], (width, width)) for c in range(4)]

        def pair(t, carry):
            for side in range(2):
                g = ext_g[source_box(b, 2 * t + side)]
                first = columns[0] - g[0:1]
                second = columns[1] - g[1:2]
                third = columns[2] - g[2:3]
                squared = first * first + second * second + third * third
                high, rest = split(lax.rsqrt(squared + columns[3] * g[3:4]))
                lanes = slice(side * width, (side + 1) * width)
                greens[b * pairs + t, :width, lanes] = high
                greens[b * pairs + t, width:, lanes] = rest
            return carry

        return lax.fori_loop(0, pairs, pair, carry)

    def near_box(b, carry):
        total = jnp.zeros((2 * q, 2 * width), F32)
        for t in range(pairs):
            source = jnp.concatenate(
                [kcat[source_box(b, 2 * t)], kcat[source_box(b, 2 * t + 1)]], axis=1
            )
            total = total + lax.dot_general(
                source, greens[b * pairs + t], (((1,), (1,)), ((), ())),
                preferred_element_type=F32,
            )
        half = total[:, :width] + total[:, width:]
        prod_ref[:, pl.ds(pl.multiple_of(b * width, width), width)] = half[:q] + half[q:]
        return carry

    fine_fwd = forward(fbuf, ff_s, ff_r)
    cuts = [nb * d // nz for d in range(nz + 1)]
    lax.fori_loop(0, cuts[1], green_box, 0)
    for d in range(1, nz):
        fine_out[d].wait_recv()
        fine_fwd[d - 1].start()
        if cuts[d + 1] > cuts[d]:
            lax.fori_loop(cuts[d], cuts[d + 1], green_box, 0)
    @pl.when(box > 0)
    def _():
        k_right.wait_recv()

    @pl.when(box < n_box - 1)
    def _():
        k_left.wait_recv()

    lax.fori_loop(0, nb, to_split, 0, unroll=4)
    lax.fori_loop(2 * nb, 3 * nb, to_split, 0, unroll=4)
    lax.fori_loop(0, nb // 2, near_box, 0, unroll=2)
    for copy in [fine_out[0]] + fine_fwd:
        copy.wait_recv()
    for i in range(n_box):
        lbuf[leaf, i] = fbuf[i, fine_rows : fine_rows + r // 2, :]
    leaf_out = [
        remote(
            lbuf.at[leaf], lbuf.at[leaf], cl_s.at[d], cl_r.at[d],
            (lax.rem(leaf + d, n_leaf), box),
        )
        for d in range(1, n_leaf)
    ]
    for copy in leaf_out:
        copy.start()
    lax.fori_loop(nb // 2, nb, near_box, 0, unroll=2)

    def open_fine(i, carry):
        for h in range(nb // 2):
            rows = fbuf[i, h * r : (h + 1) * r, :]
            fpole[i * nb + 2 * h] = rows[:, :q]
            fpole[i * nb + 2 * h + 1] = rows[:, q:]
        return carry

    lax.fori_loop(0, n_box, open_fine, 0, unroll=2)

    def open_coarse(i, carry):
        for h in range(n_leaf):
            rows = lbuf[h, i]
            cpole[h * n_box + i] = jnp.concatenate([rows[:, :q], rows[:, q:]], axis=0)
        return carry

    for copy in leaf_out:
        copy.wait_recv()
    lax.fori_loop(0, n_box, open_coarse, 0, unroll=2)

    def coupled(table, class_of, pole, index_of, live, entries):
        left_side = []
        for group in range(entries // 4):
            block = None
            for side in range(4):
                e = 4 * group + side
                mask = jnp.where(e < live, 1.0, 0.0).astype(F32)
                piece = table[class_of(e)] * mask
                block = piece if side == 0 else jnp.where(lane4 == side, piece, block)
            left_side.append(block)
        right_side = [pole[index_of(e)] for e in range(entries)]
        return nn(jnp.concatenate(left_side, axis=1), jnp.concatenate(right_side, axis=0))

    coarse_local = coupled(
        tcoarse, lambda e: cclass_ref[0, e], cpole, lambda e: clist_ref[0, e],
        ccount_ref[0], coarse_count,
    )
    lowered = nn(down_ref[...], coarse_local)
    for b in range(nb):
        dloc[b] = lowered[b * r : (b + 1) * r]

    def far_box(b, carry):
        local = dloc[b] + coupled(
            tfine, lambda e: fclass_ref[b, e], fpole,
            lambda e: jnp.clip(flist_ref[b, e] - group_first, 0, n_box * nb - 1),
            fcount_ref[b], far_count,
        )
        lanes = pl.ds(pl.multiple_of(b * width, width), width)
        prod_ref[:, lanes] = prod_ref[:, lanes] + nn(local.T, b_ref[:, lanes])
        return carry

    lax.fori_loop(0, nb, far_box, 0, unroll=4)

    stacked = jnp.concatenate([k_ref[...], prod_ref[...]], axis=0)
    gram = nt(stacked, stacked)
    share = rbuf.shape[1]
    for s in range(n_box):
        rbuf[s] = gram[s * share : (s + 1) * share]
    r_out = []
    for d in range(1, n_box):
        peer = lax.rem(box + d, n_box)
        r_out.append(
            remote(rbuf.at[peer], rrecv.at[box], r_s.at[d], r_r.at[d], (leaf, peer))
        )
        r_out[-1].start()
    rrecv[box] = rbuf[box]
    for copy in r_out:
        copy.wait_recv()
    part = rrecv[0]
    for s in range(1, n_box):
        part = part + rrecv[s]
    lrecv[leaf] = part
    l_out = []
    for d in range(1, n_leaf):
        peer = lax.rem(leaf + d, n_leaf)
        l_out.append(
            remote(lrecv.at[leaf], lrecv.at[leaf], l_s.at[d], l_r.at[d], (peer, box))
        )
        l_out[-1].start()
    for copy in l_out:
        copy.wait_recv()
    part = lrecv[0]
    for s in range(1, n_leaf):
        part = part + lrecv[s]
    gath[box] = part
    g_out = []
    for d in range(1, n_box):
        peer = lax.rem(box + d, n_box)
        g_out.append(remote(gath.at[box], gath.at[box], g_s.at[d], g_r.at[d], (leaf, peer)))
        g_out[-1].start()
    for copy in g_out:
        copy.wait_recv()
    red_ref[...] = gath[...]

    @pl.when(box < n_box - 1)
    def _():
        k_right.wait_send()
        g_right.wait_send()

    @pl.when(box > 0)
    def _():
        k_left.wait_send()
        g_left.wait_send()

    for copy in fine_out + fine_fwd + leaf_out + r_out + l_out + g_out:
        copy.wait_send()


def finish_kernel(panels, k_ref, prod_ref, red_ref, basis_ref, hess_ref, factor_ref):
    q = k_ref.shape[0]
    red = red_ref[...]
    basis_gram = red[:q, :q]
    mixed = red[:q, q:]
    mixed_t = red[q:, :q]
    image = red[q:, q:]
    inverse = 1.0 / panels
    hess = mixed * inverse
    hess_t = mixed_t * inverse
    hess_ref[...] = hess
    corrected = image - nn(mixed_t, hess) - nn(hess_t, mixed)
    corrected = (corrected + nn(nn(hess_t, basis_gram), hess)) * inverse
    eye = (
        lax.broadcasted_iota(jnp.int32, (q, q), 0) == lax.broadcasted_iota(jnp.int32, (q, q), 1)
    ).astype(F32)
    start = jnp.concatenate([corrected, eye], axis=1)
    tiles = [start[8 * t : 8 * t + 8] for t in range(q // 8)]
    row_id = lax.broadcasted_iota(jnp.int32, (8, 2 * q), 0)
    for p in range(q // 8):
        cols = [
            [jnp.broadcast_to(tiles[t][:, 8 * p + c : 8 * p + c + 1], (8, 2 * q)) for t in range(p, q // 8)]
            for c in range(8)
        ]
        for c in range(8):
            pivot = cols[c][0][c : c + 1]
            scale = lax.rsqrt(pivot)
            row = tiles[p][c : c + 1] * scale
            scaled = [tile * scale for tile in cols[c]]
            scaled[0] = jnp.where(row_id > c, scaled[0], 0.0)
            for j in range(c + 1, 8):
                value = cols[j][0][c : c + 1] * scale
                cols[j] = [x - s * value for x, s in zip(cols[j], scaled)]
            tiles[p] = jnp.where(row_id == c, row, tiles[p] - scaled[0] * row)
            for t in range(p + 1, q // 8):
                tiles[t] = tiles[t] - scaled[t - p] * row
    done = jnp.concatenate(tiles, axis=0)
    lower = done[:, :q].T
    keep = lax.broadcasted_iota(jnp.int32, (q, q), 0) >= lax.broadcasted_iota(jnp.int32, (q, q), 1)
    factor_ref[...] = jnp.where(keep, lower, 0.0)
    solve = jnp.where(keep, done[:, q:], 0.0)
    residual = prod_ref[...] - nn(hess_t, k_ref[...])
    basis_ref[...] = nn(solve, residual)


def per_device(
    krylov_block, bases, points, panel_size, panel_weight, near_list, far_list, far_class,
    far_count, coarse_list, coarse_class, coarse_count, couple_fine, couple_coarse,
    up_transfer, down_transfer,
):
    q, local = krylov_block.shape
    r = bases.shape[0]
    nb = near_list.shape[0]
    width = local // nb
    n_leaf = lax.axis_size("leaf")
    n_box = lax.axis_size("box")
    nz = n_box // 2
    share = 2 * q // n_box
    panels = local * n_leaf * n_box
    vmem = pl.BlockSpec(memory_space=pltpu.VMEM)
    smem = pl.BlockSpec(memory_space=pltpu.SMEM)
    dma = lambda n: pltpu.SemaphoreType.DMA((n,))
    product, reduced = pl.pallas_call(
        functools.partial(
            product_kernel, n_leaf, n_box, nb, width, float(width * near_list.shape[1])
        ),
        out_shape=(
            jax.ShapeDtypeStruct((q, local), F32),
            jax.ShapeDtypeStruct((n_box, share, 2 * q), F32),
        ),
        in_specs=[vmem] * 5 + [smem] * 7 + [vmem] * 4,
        out_specs=(vmem, vmem),
        scratch_shapes=[
            pltpu.VMEM((3 * nb, q, width), F32),
            pltpu.VMEM((3 * nb, 8, width), F32),
            pltpu.VMEM((3 * nb, 2 * q, width), BF16),
            pltpu.VMEM((nb, width, 8), F32),
            pltpu.VMEM((nb * (near_list.shape[1] // 2), 2 * width, 2 * width), BF16),
            pltpu.VMEM((n_box, nb // 2 * r + r // 2, 2 * q), F32),
            pltpu.VMEM((n_leaf, n_box, r // 2, 2 * q), F32),
            pltpu.VMEM((n_box * nb, r, q), F32),
            pltpu.VMEM((n_box * n_leaf, r, q), F32),
            pltpu.VMEM((couple_fine.shape[0], r, 4 * r), F32),
            pltpu.VMEM((couple_coarse.shape[0], r, 4 * r), F32),
            pltpu.VMEM((nb, r, q), F32),
            pltpu.VMEM((n_box, share, 2 * q), F32),
            pltpu.VMEM((n_box, share, 2 * q), F32),
            pltpu.VMEM((n_leaf, share, 2 * q), F32),
            pltpu.VMEM((n_box, share, 2 * q), F32),
            dma(2), dma(2), dma(2), dma(2),
            dma(nz), dma(nz), dma(nz), dma(nz),
            dma(n_leaf), dma(n_leaf),
            dma(n_box), dma(n_box), dma(n_leaf), dma(n_leaf), dma(n_box), dma(n_box),
        ],
        compiler_params=pltpu.CompilerParams(
            collective_id=0, has_side_effects=True, vmem_limit_bytes=63 * 2**20
        ),
    )(
        krylov_block, bases, points, panel_size[None, :], panel_weight[None, :],
        near_list, far_list, far_class, far_count, coarse_list, coarse_class, coarse_count,
        couple_fine, couple_coarse,
        up_transfer.reshape(-1, r), down_transfer.reshape(-1, r),
    )
    return pl.pallas_call(
        functools.partial(finish_kernel, float(panels)),
        out_shape=(
            jax.ShapeDtypeStruct((q, local), F32),
            jax.ShapeDtypeStruct((q, q), F32),
            jax.ShapeDtypeStruct((q, q), F32),
        ),
        in_specs=[vmem] * 3,
        out_specs=(vmem, vmem, vmem),
        compiler_params=pltpu.CompilerParams(vmem_limit_bytes=63 * 2**20),
    )(krylov_block, product, reduced.reshape(2 * q, 2 * q))


def solution(mesh):
    split_last = P(None, ("leaf", "box"))
    split_first = P(("leaf", "box"), None)
    flat = P(("leaf", "box"))
    in_specs = (
        split_last, split_last, split_last, flat, flat,
        split_first, split_first, split_first, flat,
        split_first, split_first, flat,
        P(), P(), P(), P(),
    )
    return jax.shard_map(
        per_device, mesh=mesh, in_specs=in_specs, out_specs=(split_last, P(), P()),
        check_vma=False,
    )
```
